256 devices in a mesh: lat: 8 (over y_lo, x), lon: 32 (over y_hi, z, core).
Axes of the slice: x: 4, y: 4 (y_hi: 2, y_lo: 2; y = y_hi * 2 + y_lo), z: 8, core: 2. Of those that a mesh axis runs over, the one named last changes fastest.
Arguments:
- adj_arrival: float32 [256, 2048, 512], P('lat', 'lon'), may hold values from -6 to 6
- weights: float32 [256, 2048, 16], P('lat', 'lon'), may hold values from -1.5 to 1.5
- dep_lat: int32 [256, 2048], P('lat', 'lon'), may hold values from -6 to 6
- dep_lon: int32 [256, 2048], P('lat', 'lon'), may hold values from -6 to 6
Outputs:
- adj_departure: float32 [256, 2048, 512], P('lat', 'lon')
The draws below stay inside these ranges and needn't reach their ends.
All inputs are finite; a program needn't handle non-finite values.
Results may differ from the reference program's by a relative error of at most 0.00007.
Values sent between devices are 32-bit elements; how exact they have to be, the bound alone decides.
A program may use at most 320 MiB of HBM per device.

```python
import jax
import jax.numpy as jnp
from jax import lax

REACH = 6
FIELDS = 512
NLAT = 256
NLON = 2048


def plant(values, rng, low, top_value):
    index_at = [jax.random.randint(jax.random.fold_in(rng, axis), (), 0, length) for axis, length in enumerate(values.shape)]
    main_axis = values.shape.index(max(values.shape))
    beside = index_at[:main_axis] + [(index_at[main_axis] + 1) % values.shape[main_axis]] + index_at[main_axis + 1:]
    return values.at[tuple(index_at)].set(low).at[tuple(beside)].set(top_value)


def block_scale(own_key, dims, cuts, low, top_value):
    def one(position, parts):
        draws = jax.random.uniform(jax.random.fold_in(jax.random.fold_in(own_key, 6), position), (parts,), jnp.float32, low / len(cuts), top_value / len(cuts))
        return jnp.repeat(jnp.exp(draws), dims[position] // parts).reshape((-1,) + (1,) * (len(dims) - position - 1))

    factor_of = one(*cuts[0])
    for cut in cuts[1:]:
        factor_of = factor_of * one(*cut)
    return factor_of


def gaussian(own_key, dims, deviation, most, split=(), kind=jnp.bfloat16):
    values = jax.random.normal(own_key, dims, jnp.float32) * deviation
    if len(split) > 0:
        values = block_scale(own_key, dims, split, -0.22, 0.18) * values
    return jnp.clip(values, min=-most, max=most).astype(kind)


def setup_inputs(seed: int = 0) -> dict:
    key_of = jax.random.split(jax.random.key(seed), 5)
    return {
        "adj_arrival": gaussian(key_of[0], (NLAT, NLON, FIELDS), 1.0, 6.0, ((0, 8), (1, 32)), jnp.float32),
        "weights": gaussian(key_of[1], (NLAT, NLON, 16), 0.25, 1.5, ((0, 8), (1, 32)), jnp.float32),
        "dep_lat": plant(jax.random.randint(key_of[2], (NLAT, NLON), 0 - REACH, REACH + 1), jax.random.fold_in(key_of[2], 1), 0 - REACH, REACH).astype(jnp.int32),
        "dep_lon": plant(jax.random.randint(key_of[3], (NLAT, NLON), 0 - REACH, REACH + 1), jax.random.fold_in(key_of[3], 1), 0 - REACH, REACH).astype(jnp.int32),
    }


def reference(adj_arrival, weights, dep_lat, dep_lon):
    nrows, ncols, fields = adj_arrival.shape
    rows_idx = lax.broadcasted_iota(jnp.int32, (nrows, ncols), 0)
    cols_idx = lax.broadcasted_iota(jnp.int32, (nrows, ncols), 1)
    flat_values = adj_arrival.reshape(nrows * ncols, fields)
    buffer = jnp.zeros((nrows * ncols + 1, fields), jnp.float32)
    dump_row = jnp.int32(nrows * ncols)
    for step_a in range(4):
        for step_b in range(4):
            target_row = (rows_idx + dep_lat + step_a - 1).astype(jnp.int32)
            target_col = ((cols_idx + dep_lon + step_b - 1) % ncols).astype(jnp.int32)
            inside = (target_row >= 0) & (target_row < nrows)
            target = jnp.where(inside, target_row * ncols + target_col, dump_row).reshape(-1)
            scaled = weights[:, :, 4 * step_a + step_b].reshape(-1, 1) * flat_values
            buffer = buffer.at[target].add(scaled)
    return buffer[:-1].reshape(nrows, ncols, fields)
```

```python
import functools

import jax
import jax.numpy as jnp
from jax import lax
from jax.experimental import pallas as pl
from jax.experimental.pallas import tpu as pltpu
from jax.sharding import PartitionSpec as P

NROWS, NCOLS, FIELDS = 32, 64, 512
HALO = 8
WIDE = NCOLS + 2 * HALO
GROUP = 4
KEYS = GROUP * NCOLS
HALF = 256
MESH = pl.DeviceIdType.MESH
f32, bf16, i32 = jnp.float32, jnp.bfloat16, jnp.int32


def kernel(v_hbm, w_hbm, da_hbm, db_hbm, out_hbm, lon_hbm,
           v, w, da, db, acc, coef, rhs, lat_send, lat_recv, lon_send, lon_recv, own_sem):
    nlat, nlon = lax.axis_size("lat"), lax.axis_size("lon")
    la, lo = lax.axis_index("lat"), lax.axis_index("lon")
    has_south, has_north = la > 0, la < nlat - 1
    south, north = {"lat": jnp.maximum(la - 1, 0)}, {"lat": jnp.minimum(la + 1, nlat - 1)}
    east, west = {"lon": lax.rem(lo + 1, nlon)}, {"lon": lax.rem(lo + nlon - 1, nlon)}

    barrier = pltpu.get_barrier_semaphore()
    pl.semaphore_signal(barrier, inc=1, device_id=east, device_id_type=MESH)
    pl.semaphore_signal(barrier, inc=1, device_id=west, device_id_type=MESH)

    @pl.when(has_north)
    def _():
        pl.semaphore_signal(barrier, inc=1, device_id=north, device_id_type=MESH)

    @pl.when(has_south)
    def _():
        pl.semaphore_signal(barrier, inc=1, device_id=south, device_id_type=MESH)

    own = [
        pltpu.make_async_copy(v_hbm, v.at[HALO:HALO + NROWS], own_sem.at[0]),
        pltpu.make_async_copy(w_hbm, w.at[HALO:HALO + NROWS], own_sem.at[1]),
        pltpu.make_async_copy(da_hbm, da.at[HALO:HALO + NROWS], own_sem.at[2]),
        pltpu.make_async_copy(db_hbm, db.at[HALO:HALO + NROWS], own_sem.at[3]),
    ]
    for copy in own:
        copy.start()
    pl.semaphore_wait(barrier, 2 + has_north.astype(i32) + has_south.astype(i32))

    def to(device, src, dst, sems, k):
        return pltpu.make_async_remote_copy(
            src_ref=src, dst_ref=dst, send_sem=sems[0].at[k], recv_sem=sems[1].at[k],
            device_id=device, device_id_type=MESH)

    lat = (lat_send, lat_recv)
    far = HALO + NROWS
    northward = [
        to(north, w_hbm.at[24:32], w.at[0:8], lat, 0),
        to(north, da_hbm.at[24:32], da.at[0:8], lat, 1),
        to(north, db_hbm.at[24:32], db.at[0:8], lat, 2),
        to(north, v_hbm.at[28:32], v.at[4:8], lat, 3),
        to(north, v_hbm.at[24:28], v.at[0:4], lat, 4),
    ]
    southward = [
        to(south, w_hbm.at[0:8], w.at[far:far + 8], lat, 5),
        to(south, da_hbm.at[0:8], da.at[far:far + 8], lat, 6),
        to(south, db_hbm.at[0:8], db.at[far:far + 8], lat, 7),
        to(south, v_hbm.at[0:4], v.at[far:far + 4], lat, 8),
        to(south, v_hbm.at[4:7], v.at[far + 4:far + 7], lat, 9),
    ]

    @pl.when(has_north)
    def _():
        for copy in northward:
            copy.start()

    @pl.when(has_south)
    def _():
        for copy in southward:
            copy.start()

    v[far + 7] = jnp.zeros((NCOLS, FIELDS), f32)
    acc[...] = jnp.zeros_like(acc)
    for copy in own:
        copy.wait()

    lane = lax.broadcasted_iota(i32, (1, KEYS), 1)
    col_of, row_of = lane % NCOLS, lane // NCOLS

    def deposit(first, start, size):
        def rows(ref):
            return jnp.concatenate([ref[pl.ds(first + k, 1), :] for k in range(GROUP)], axis=1)
        values = v[pl.ds(first, GROUP)].reshape(KEYS, FIELDS)
        high = values.astype(bf16)
        rhs[0:KEYS] = high
        rhs[KEYS:2 * KEYS] = (values - high.astype(f32)).astype(bf16)
        weights = jnp.concatenate([w[first + k] for k in range(GROUP)], axis=1)
        column = lax.broadcasted_iota(i32, (WIDE, KEYS), 0) - (col_of + rows(db) + (HALO - 1))
        at = [column == b for b in range(4)]
        highs, lows = [], []
        for a in range(4):
            g = jnp.zeros((WIDE, KEYS), f32)
            for b in range(4):
                g = jnp.where(at[b], weights[4 * a + b:4 * a + b + 1], g)
            h = g.astype(bf16)
            highs.append(h)
            lows.append((g - h.astype(f32)).astype(bf16))
        base = start - (row_of + rows(da) + (first - HALO - 1))
        for t in range(size):
            step = base + t
            pick = [jnp.broadcast_to((step == a).astype(f32), (16, KEYS)).astype(bf16) for a in range(4)]
            pick = [jnp.concatenate([p] * (WIDE // 16), axis=0) for p in pick]
            place = slice(t * WIDE, (t + 1) * WIDE)
            coef[place, 0:KEYS] = sum(p * g for p, g in zip(pick, highs))
            coef[place, KEYS:2 * KEYS] = sum(p * g for p, g in zip(pick, lows))
        tall = slice(0, size * WIDE)
        for n in range(FIELDS // HALF):
            part = slice(n * HALF, (n + 1) * HALF)
            ch, cl = coef[tall, 0:KEYS], coef[tall, KEYS:2 * KEYS]
            c = jnp.concatenate([ch, cl, ch], axis=1)
            rh, rl = rhs[0:KEYS, part], rhs[KEYS:2 * KEYS, part]
            r = jnp.concatenate([rh, rh, rl], axis=0)
            out = jnp.dot(c, r, preferred_element_type=f32)
            acc[pl.ds(start, size), :, part] += out.reshape(size, WIDE, HALF)

    @pl.loop(0, 4)
    def _(k):
        deposit(HALO + 8 + 4 * k, 1 + 4 * k, 19)

    @pl.loop(0, 2)
    def _(k):
        deposit(HALO + 4 + 20 * k, 16 * k, 16)

    @pl.loop(0, 2)
    def _(k):
        deposit(HALO + 28 * k, 20 * k, 12)

    lon = (lon_send, lon_recv)

    def sides(first, count, k):
        return [
            to(west, acc.at[first:first + count, 0:HALO], lon_hbm.at[1, first:first + count], lon, k),
            to(east, acc.at[first:first + count, WIDE - HALO:WIDE], lon_hbm.at[0, first:first + count], lon, k + 1),
        ]

    sideward = [sides(8, 16, 0), sides(4, 4, 2), sides(24, 4, 4), sides(0, 4, 6), sides(28, 4, 8)]
    for copy in sideward[0]:
        copy.start()

    @pl.when(has_south)
    def _():
        for copy in northward[:4]:
            copy.wait_recv()

    @pl.when(has_north)
    def _():
        for copy in southward[:4]:
            copy.wait_recv()

    @pl.loop(0, 2)
    def _(k):
        @pl.when(jnp.logical_or(jnp.logical_and(k == 0, has_south), jnp.logical_and(k == 1, has_north)))
        def _():
            deposit(4 + (far - 4) * k, 24 * k, 8)

    for copy in sideward[1] + sideward[2]:
        copy.start()

    @pl.when(has_south)
    def _():
        northward[4].wait_recv()

    @pl.when(has_north)
    def _():
        southward[4].wait_recv()

    @pl.loop(0, 2)
    def _(k):
        @pl.when(jnp.logical_or(jnp.logical_and(k == 0, has_south), jnp.logical_and(k == 1, has_north)))
        def _():
            deposit((far + 4) * k, 28 * k, 4)

    for copy in sideward[3] + sideward[4]:
        copy.start()
    result = pltpu.make_async_copy(acc.at[:, HALO:HALO + NCOLS], out_hbm, own_sem.at[0])
    result.start()

    @pl.when(has_north)
    def _():
        for copy in northward:
            copy.wait_send()

    @pl.when(has_south)
    def _():
        for copy in southward:
            copy.wait_send()

    for pair in sideward:
        for copy in pair:
            copy.wait()
    result.wait()


def body(adj_arrival, weights, dep_lat, dep_lon):
    by_point = jnp.transpose(weights, (0, 2, 1))
    hbm = pl.BlockSpec(memory_space=pl.ANY)
    ext = NROWS + 2 * HALO
    middle, lon = pl.pallas_call(
        kernel,
        out_shape=(
            jax.ShapeDtypeStruct((NROWS, NCOLS, FIELDS), f32),
            jax.ShapeDtypeStruct((2, NROWS, HALO, FIELDS), f32),
        ),
        in_specs=[hbm] * 4,
        out_specs=(hbm, hbm),
        scratch_shapes=[
            pltpu.VMEM((ext, NCOLS, FIELDS), f32),
            pltpu.VMEM((ext, 16, NCOLS), f32),
            pltpu.VMEM((ext, NCOLS), i32),
            pltpu.VMEM((ext, NCOLS), i32),
            pltpu.VMEM((NROWS, WIDE, FIELDS), f32),
            pltpu.VMEM((19 * WIDE, 2 * KEYS), bf16),
            pltpu.VMEM((2 * KEYS, FIELDS), bf16),
            pltpu.SemaphoreType.DMA((10,)),
            pltpu.SemaphoreType.DMA((10,)),
            pltpu.SemaphoreType.DMA((10,)),
            pltpu.SemaphoreType.DMA((10,)),
            pltpu.SemaphoreType.DMA((4,)),
        ],
        compiler_params=pltpu.CompilerParams(
            collective_id=0, has_side_effects=True, vmem_limit_bytes=58 << 20),
    )(adj_arrival, by_point, dep_lat, dep_lon)
    return jnp.concatenate(
        [middle[:, :HALO] + lon[0], middle[:, HALO:NCOLS - HALO], middle[:, NCOLS - HALO:] + lon[1]], axis=1)


def solution(mesh):
    placed = (P("lat", "lon", None), P("lat", "lon", None), P("lat", "lon"), P("lat", "lon"))
    return jax.shard_map(
        body, mesh=mesh, in_specs=placed, out_specs=P("lat", "lon", None), check_vma=False
    )
```

```python
import jax
import jax.numpy as jnp
from jax import lax
from jax.experimental import pallas as pl
from jax.experimental.pallas import tpu as pltpu
from jax.sharding import PartitionSpec as P

NROWS, NCOLS, FIELDS = 32, 64, 512
HALO = 8
FAR = HALO + NROWS
EXT = FAR + HALO
GROUP = 4
KEYS = GROUP * NCOLS
EDGE_GROUP = 16
HALF = 256
MESH = pl.DeviceIdType.MESH
f32, bf16, i32 = jnp.float32, jnp.bfloat16, jnp.int32


def kernel(v_hbm, w_hbm, da_hbm, db_hbm, out_hbm,
           v, w, da, db, acc, side, side_in, relay, coef, rhs,
           lat_send, lat_recv, hop_send, hop_recv, lon_send, lon_recv, own_sem, out_sem):
    nlat, nlon = lax.axis_size("lat"), lax.axis_size("lon")
    half_lat = nlat // 2
    la, lo = lax.axis_index("lat"), lax.axis_index("lon")
    has_south, has_north = la > 0, la < nlat - 1
    at_first, at_last = la == 0, la == nlat - 1
    below, above = la == half_lat - 1, la == half_lat
    at_end, at_middle = jnp.logical_or(at_first, at_last), jnp.logical_or(below, above)
    south, north = {"lat": jnp.maximum(la - 1, 0)}, {"lat": jnp.minimum(la + 1, nlat - 1)}
    east, west = {"lon": lax.rem(lo + 1, nlon)}, {"lon": lax.rem(lo + nlon - 1, nlon)}
    first, last = {"lat": jnp.int32(0)}, {"lat": jnp.int32(nlat - 1)}
    lower, upper = {"lat": jnp.int32(half_lat - 1)}, {"lat": jnp.int32(half_lat)}

    barrier = pltpu.get_barrier_semaphore()

    def greet(device):
        pl.semaphore_signal(barrier, inc=1, device_id=device, device_id_type=MESH)

    greet(east)
    greet(west)

    @pl.when(has_north)
    def _():
        greet(north)

    @pl.when(has_south)
    def _():
        greet(south)

    @pl.when(at_end)
    def _():
        greet(lower)
        greet(upper)

    @pl.when(at_middle)
    def _():
        greet(first)
        greet(last)

    own = [
        pltpu.make_async_copy(v_hbm, v.at[HALO:FAR], own_sem.at[0]),
        pltpu.make_async_copy(w_hbm, w.at[HALO:FAR], own_sem.at[1]),
        pltpu.make_async_copy(da_hbm, da.at[HALO:FAR], own_sem.at[2]),
        pltpu.make_async_copy(db_hbm, db.at[HALO:FAR], own_sem.at[3]),
    ]
    for copy in own:
        copy.start()
    pl.semaphore_wait(
        barrier,
        2 + has_north.astype(i32) + has_south.astype(i32) + 2 * at_end.astype(i32) + 2 * at_middle.astype(i32))

    def to(device, src, dst, sems, k):
        return pltpu.make_async_remote_copy(
            src_ref=src, dst_ref=dst, send_sem=sems[0].at[k], recv_sem=sems[1].at[k],
            device_id=device, device_id_type=MESH)

    lat, hop, lon = (lat_send, lat_recv), (hop_send, hop_recv), (lon_send, lon_recv)
    mid = slice(HALO, NCOLS - HALO)
    left, right = slice(0, HALO), slice(NCOLS - HALO, NCOLS)
    northward = [
        to(north, v_hbm.at[24:32, left], v.at[0:8, left], lat, 0),
        to(north, v_hbm.at[24:32, right], v.at[0:8, right], lat, 1),
        to(north, w_hbm.at[24:32], w.at[0:8], lat, 2),
        to(north, da_hbm.at[24:32], da.at[0:8], lat, 3),
        to(north, db_hbm.at[24:32], db.at[0:8], lat, 4),
        to(north, v_hbm.at[28:32, mid], v.at[4:8, mid], lat, 5),
    ]
    north_far = to(north, v_hbm.at[24:28, mid], v.at[0:4, mid], lat, 6)
    southward = [
        to(south, v_hbm.at[0:7, left], v.at[FAR:FAR + 7, left], lat, 7),
        to(south, v_hbm.at[0:7, right], v.at[FAR:FAR + 7, right], lat, 8),
        to(south, w_hbm.at[0:8], w.at[FAR:FAR + 8], lat, 9),
        to(south, da_hbm.at[0:8], da.at[FAR:FAR + 8], lat, 10),
        to(south, db_hbm.at[0:8], db.at[FAR:FAR + 8], lat, 11),
        to(south, v_hbm.at[0:4, mid], v.at[FAR:FAR + 4, mid], lat, 12),
    ]
    south_far = to(south, v_hbm.at[4:7, mid], v.at[FAR + 4:FAR + 7, mid], lat, 13)
    hop_north = [
        to(last, v_hbm.at[26:28, mid], relay.at[2:4], hop, 0),
        to(last, v_hbm.at[24:26, mid], relay.at[0:2], hop, 1),
    ]
    on_north = [
        to(upper, relay.at[2:4], v.at[2:4, mid], hop, 2),
        to(upper, relay.at[0:2], v.at[0:2, mid], hop, 3),
    ]
    hop_south = [
        to(first, v_hbm.at[4:6, mid], relay.at[0:2], hop, 4),
        to(first, v_hbm.at[6:7, mid], relay.at[2:3], hop, 5),
    ]
    on_south = [
        to(lower, relay.at[0:2], v.at[FAR + 4:FAR + 6, mid], hop, 6),
        to(lower, relay.at[2:3], v.at[FAR + 6:FAR + 7, mid], hop, 7),
    ]

    @pl.when(below)
    def _():
        for copy in hop_north:
            copy.start()

    @pl.when(above)
    def _():
        for copy in hop_south:
            copy.start()

    @pl.when(has_north)
    def _():
        for copy in northward:
            copy.start()

    @pl.when(has_south)
    def _():
        for copy in southward:
            copy.start()

    @pl.when(jnp.logical_and(has_north, jnp.logical_not(below)))
    def _():
        north_far.start()

    @pl.when(jnp.logical_and(has_south, jnp.logical_not(above)))
    def _():
        south_far.start()

    v[EXT - 1] = jnp.zeros((NCOLS, FIELDS), f32)

    @pl.when(at_first)
    def _():
        v[0:HALO] = jnp.zeros((HALO, NCOLS, FIELDS), f32)
        w[0:HALO] = jnp.zeros((HALO, 16, NCOLS), f32)
        da[0:HALO] = jnp.zeros((HALO, NCOLS), i32)
        db[0:HALO] = jnp.zeros((HALO, NCOLS), i32)

    @pl.when(at_last)
    def _():
        v[FAR:EXT - 1] = jnp.zeros((HALO - 1, NCOLS, FIELDS), f32)
        w[FAR:EXT] = jnp.zeros((HALO, 16, NCOLS), f32)
        da[FAR:EXT] = jnp.zeros((HALO, NCOLS), i32)
        db[FAR:EXT] = jnp.zeros((HALO, NCOLS), i32)

    acc[...] = jnp.zeros_like(acc)
    side[...] = jnp.zeros_like(side)
    for copy in own:
        copy.wait()

    lane = lax.broadcasted_iota(i32, (1, KEYS), 1)

    def split(values):
        high = values.astype(bf16)
        return high, (values - high.astype(f32)).astype(bf16)

    def multiply(total, start, size, width, values):
        rhs[0:KEYS], rhs[KEYS:2 * KEYS] = split(values)
        tall = slice(0, size * width)
        for n in range(FIELDS // HALF):
            part = slice(n * HALF, (n + 1) * HALF)
            c = jnp.concatenate([coef[tall, 0:KEYS], coef[tall, KEYS:2 * KEYS], coef[tall, 0:KEYS]], axis=1)
            r = jnp.concatenate([rhs[0:KEYS, part], rhs[0:KEYS, part], rhs[KEYS:2 * KEYS, part]], axis=0)
            out = jnp.dot(c, r, preferred_element_type=f32)
            total[pl.ds(start, size), :, part] += out.reshape(size, width, HALF)

    def place_rows(base, size, width, highs, lows):
        for t in range(size):
            pick = [jnp.broadcast_to((base == t - a).astype(f32), (16, KEYS)).astype(bf16) for a in range(4)]
            pick = [jnp.concatenate([p] * (width // 16), axis=0) for p in pick]
            place = slice(t * width, (t + 1) * width)
            coef[place, 0:KEYS] = sum(p * g for p, g in zip(pick, highs))
            coef[place, KEYS:2 * KEYS] = sum(p * g for p, g in zip(pick, lows))

    def deposit(source, start, size):
        def rows(ref):
            return jnp.concatenate([ref[pl.ds(source + k, 1), :] for k in range(GROUP)], axis=1)
        weights = jnp.concatenate([w[source + k] for k in range(GROUP)], axis=1)
        column = lax.broadcasted_iota(i32, (NCOLS, KEYS), 0) - (lane % NCOLS + rows(db) - 1)
        at = [column == b for b in range(4)]
        highs, lows = [], []
        for a in range(4):
            g = jnp.zeros((NCOLS, KEYS), f32)
            for b in range(4):
                g = jnp.where(at[b], weights[4 * a + b:4 * a + b + 1], g)
            h, low = split(g)
            highs.append(h)
            lows.append(low)
        base = lane // NCOLS + rows(da) + (source - HALO - 1) - start
        place_rows(base, size, NCOLS, highs, lows)
        multiply(acc, start, size, NCOLS, v[pl.ds(source, GROUP)].reshape(KEYS, FIELDS))

    def deposit_sides(source, start, size):
        many = EDGE_GROUP * NCOLS

        def rows(ref):
            joined = jnp.concatenate([ref[source + k:source + k + 1, :] for k in range(EDGE_GROUP)], axis=1)
            return jnp.broadcast_to(joined.astype(f32), (16, many)).astype(bf16)
        high, low = split(jnp.concatenate([w[source + k] for k in range(EDGE_GROUP)], axis=1))
        stacked = jnp.concatenate([high, low, rows(da), rows(db)], axis=0)
        row_of, col_of = lane % 128 // 8, lane % 8 + (NCOLS - HALO) * (lane // 128)
        chosen = (lax.broadcasted_iota(i32, (many, KEYS), 0) == row_of * NCOLS + col_of).astype(f32).astype(bf16)
        packed = jnp.dot(stacked, chosen, preferred_element_type=f32)
        step_a, step_b = packed[32:33].astype(i32), packed[48:49].astype(i32)
        target = lax.broadcasted_iota(i32, (16, KEYS), 0)
        target = jnp.where(target < HALO, target - HALO, target + (NCOLS - HALO))
        column = target - (col_of + step_b - 1)
        at = [column == b for b in range(4)]
        kept = []
        for part in (0, 16):
            for a in range(4):
                g = jnp.zeros((16, KEYS), f32)
                for b in range(4):
                    g = jnp.where(at[b], packed[part + 4 * a + b:part + 4 * a + b + 1], g)
                kept.append(g.astype(bf16))
        base = row_of + step_a + (source - HALO - 1) - start
        place_rows(base, size, 16, kept[:4], kept[4:])
        near = slice(source, source + EDGE_GROUP)
        values = jnp.concatenate(
            [v[near, left].reshape(KEYS // 2, FIELDS), v[near, right].reshape(KEYS // 2, FIELDS)], axis=0)
        multiply(side, start, size, 16, values)

    deposit_sides(HALO + 8, 1, 31)

    @pl.loop(0, 4)
    def _(k):
        deposit(HALO + 8 + 4 * k, 1 + 4 * k, 19)

    @pl.when(at_last)
    def _():
        for here, onward in zip(hop_north, on_north):
            here.wait_recv()
            onward.start()

    @pl.when(at_first)
    def _():
        for here, onward in zip(hop_south, on_south):
            here.wait_recv()
            onward.start()

    @pl.when(has_south)
    def _():
        for copy in northward[:5]:
            copy.wait_recv()

    @pl.when(has_north)
    def _():
        for copy in southward[:5]:
            copy.wait_recv()

    deposit_sides(0, 0, 16)
    deposit_sides(HALO + 24, 17, 15)
    sideward = [
        to(west, side.at[:, 0:HALO], side_in.at[1], lon, 0),
        to(east, side.at[:, HALO:2 * HALO], side_in.at[0], lon, 1),
    ]
    for copy in sideward:
        copy.start()

    @pl.loop(0, 2)
    def _(k):
        deposit(HALO + 4 + 20 * k, 16 * k, 16)

    @pl.loop(0, 2)
    def _(k):
        deposit(HALO + 28 * k, 20 * k, 12)

    for copy in sideward:
        copy.wait_recv()
    acc[:, left] += side_in[0]
    acc[:, right] += side_in[1]

    def write(source, count, k):
        copy = pltpu.make_async_copy(
            acc.at[source:source + count], out_hbm.at[source:source + count], out_sem.at[k])
        copy.start()
        return copy

    written = [write(8, 16, 0)]

    @pl.when(has_south)
    def _():
        northward[5].wait_recv()

    @pl.when(has_north)
    def _():
        southward[5].wait_recv()

    def one_has(k):
        return jnp.logical_or(jnp.logical_and(k == 0, has_south), jnp.logical_and(k == 1, has_north))

    @pl.loop(0, 2)
    def _(k):
        @pl.when(one_has(k))
        def _():
            deposit(4 + (FAR - 4) * k, 24 * k, 8)

    written += [write(4, 4, 1), write(24, 4, 2)]

    @pl.when(jnp.logical_and(has_south, jnp.logical_not(above)))
    def _():
        north_far.wait_recv()

    @pl.when(above)
    def _():
        for copy in on_north:
            copy.wait_recv()

    @pl.when(jnp.logical_and(has_north, jnp.logical_not(below)))
    def _():
        south_far.wait_recv()

    @pl.when(below)
    def _():
        for copy in on_south:
            copy.wait_recv()

    @pl.loop(0, 2)
    def _(k):
        @pl.when(one_has(k))
        def _():
            deposit((FAR + 4) * k, 28 * k, 4)

    written += [write(0, 4, 3), write(28, 4, 4)]

    @pl.when(has_north)
    def _():
        for copy in northward:
            copy.wait_send()

    @pl.when(has_south)
    def _():
        for copy in southward:
            copy.wait_send()

    @pl.when(jnp.logical_and(has_north, jnp.logical_not(below)))
    def _():
        north_far.wait_send()

    @pl.when(jnp.logical_and(has_south, jnp.logical_not(above)))
    def _():
        south_far.wait_send()

    @pl.when(below)
    def _():
        for copy in hop_north:
            copy.wait_send()

    @pl.when(above)
    def _():
        for copy in hop_south:
            copy.wait_send()

    @pl.when(at_last)
    def _():
        for copy in on_north:
            copy.wait_send()

    @pl.when(at_first)
    def _():
        for copy in on_south:
            copy.wait_send()

    for copy in sideward:
        copy.wait_send()
    for copy in written:
        copy.wait()


def body(adj_arrival, weights, dep_lat, dep_lon):
    by_point = jnp.transpose(weights, (0, 2, 1))
    hbm = pl.BlockSpec(memory_space=pl.ANY)
    dma = pltpu.SemaphoreType.DMA
    return pl.pallas_call(
        kernel,
        out_shape=jax.ShapeDtypeStruct((NROWS, NCOLS, FIELDS), f32),
        in_specs=[hbm] * 4,
        out_specs=hbm,
        scratch_shapes=[
            pltpu.VMEM((EXT, NCOLS, FIELDS), f32),
            pltpu.VMEM((EXT, 16, NCOLS), f32),
            pltpu.VMEM((EXT, NCOLS), i32),
            pltpu.VMEM((EXT, NCOLS), i32),
            pltpu.VMEM((NROWS, NCOLS, FIELDS), f32),
            pltpu.VMEM((NROWS, 2 * HALO, FIELDS), f32),
            pltpu.VMEM((2, NROWS, HALO, FIELDS), f32),
            pltpu.VMEM((GROUP, NCOLS - 2 * HALO, FIELDS), f32),
            pltpu.VMEM((19 * NCOLS, 2 * KEYS), bf16),
            pltpu.VMEM((2 * KEYS, FIELDS), bf16),
            dma((14,)), dma((14,)), dma((8,)), dma((8,)), dma((2,)), dma((2,)), dma((4,)), dma((5,)),
        ],
        compiler_params=pltpu.CompilerParams(
            collective_id=0, has_side_effects=True, vmem_limit_bytes=58 << 20),
    )(adj_arrival, by_point, dep_lat, dep_lon)


def solution(mesh):
    placed = (P("lat", "lon", None), P("lat", "lon", None), P("lat", "lon"), P("lat", "lon"))
    return jax.shard_map(
        body, mesh=mesh, in_specs=placed, out_specs=P("lat", "lon", None), check_vma=False
    )
```

```python
import jax
import jax.numpy as jnp
from jax import lax
from jax.experimental import pallas as pl
from jax.experimental.pallas import tpu as pltpu
from jax.sharding import PartitionSpec as P

NROWS, NCOLS, FIELDS = 32, 64, 512
HALO = 8
FAR = HALO + NROWS
EXT = FAR + HALO
GROUP = 4
KEYS = GROUP * NCOLS
EDGE_GROUP = 16
HALF = 256
MESH = pl.DeviceIdType.MESH
f32, bf16, i32 = jnp.float32, jnp.bfloat16, jnp.int32


def kernel(v_hbm, w_hbm, da_hbm, db_hbm, out_hbm,
           v, w, da, db, acc, side, side_in, relay, coef, rhs,
           lat_send, lat_recv, hop_send, hop_recv, lon_send, lon_recv, own_sem, out_sem):
    nlat, nlon = lax.axis_size("lat"), lax.axis_size("lon")
    half_lat = nlat // 2
    la, lo = lax.axis_index("lat"), lax.axis_index("lon")
    has_south, has_north = la > 0, la < nlat - 1
    at_first, at_last = la == 0, la == nlat - 1
    below, above = la == half_lat - 1, la == half_lat
    at_end, at_middle = jnp.logical_or(at_first, at_last), jnp.logical_or(below, above)
    south, north = {"lat": jnp.maximum(la - 1, 0)}, {"lat": jnp.minimum(la + 1, nlat - 1)}
    east, west = {"lon": lax.rem(lo + 1, nlon)}, {"lon": lax.rem(lo + nlon - 1, nlon)}
    first, last = {"lat": jnp.int32(0)}, {"lat": jnp.int32(nlat - 1)}
    lower, upper = {"lat": jnp.int32(half_lat - 1)}, {"lat": jnp.int32(half_lat)}

    barrier = pltpu.get_barrier_semaphore()

    def greet(device):
        pl.semaphore_signal(barrier, inc=1, device_id=device, device_id_type=MESH)

    greet(east)
    greet(west)

    @pl.when(has_north)
    def _():
        greet(north)

    @pl.when(has_south)
    def _():
        greet(south)

    @pl.when(at_end)
    def _():
        greet(lower)
        greet(upper)

    @pl.when(at_middle)
    def _():
        greet(first)
        greet(last)

    own = [
        pltpu.make_async_copy(v_hbm, v.at[HALO:FAR], own_sem.at[0]),
        pltpu.make_async_copy(w_hbm, w.at[HALO:FAR], own_sem.at[1]),
        pltpu.make_async_copy(da_hbm, da.at[HALO:FAR], own_sem.at[2]),
        pltpu.make_async_copy(db_hbm, db.at[HALO:FAR], own_sem.at[3]),
    ]
    for copy in own:
        copy.start()
    pl.semaphore_wait(
        barrier,
        2 + has_north.astype(i32) + has_south.astype(i32) + 2 * at_end.astype(i32) + 2 * at_middle.astype(i32))

    def to(device, src, dst, sems, k):
        return pltpu.make_async_remote_copy(
            src_ref=src, dst_ref=dst, send_sem=sems[0].at[k], recv_sem=sems[1].at[k],
            device_id=device, device_id_type=MESH)

    lat, hop, lon = (lat_send, lat_recv), (hop_send, hop_recv), (lon_send, lon_recv)
    mid = slice(HALO, NCOLS - HALO)
    left, right = slice(0, HALO), slice(NCOLS - HALO, NCOLS)
    northward = [
        to(north, v_hbm.at[24:32, left], v.at[0:8, left], lat, 0),
        to(north, v_hbm.at[24:32, right], v.at[0:8, right], lat, 1),
        to(north, w_hbm.at[24:32], w.at[0:8], lat, 2),
        to(north, da_hbm.at[24:32], da.at[0:8], lat, 3),
        to(north, db_hbm.at[24:32], db.at[0:8], lat, 4),
        to(north, v_hbm.at[28:32, mid], v.at[4:8, mid], lat, 5),
    ]
    north_far = to(north, v_hbm.at[24:28, mid], v.at[0:4, mid], lat, 6)
    southward = [
        to(south, v_hbm.at[0:7, left], v.at[FAR:FAR + 7, left], lat, 7),
        to(south, v_hbm.at[0:7, right], v.at[FAR:FAR + 7, right], lat, 8),
        to(south, w_hbm.at[0:8], w.at[FAR:FAR + 8], lat, 9),
        to(south, da_hbm.at[0:8], da.at[FAR:FAR + 8], lat, 10),
        to(south, db_hbm.at[0:8], db.at[FAR:FAR + 8], lat, 11),
        to(south, v_hbm.at[0:4, mid], v.at[FAR:FAR + 4, mid], lat, 12),
    ]
    south_far = to(south, v_hbm.at[4:7, mid], v.at[FAR + 4:FAR + 7, mid], lat, 13)
    hop_north = [
        to(last, v_hbm.at[26:28, mid], relay.at[2:4], hop, 0),
        to(last, v_hbm.at[24:26, mid], relay.at[0:2], hop, 1),
    ]
    on_north = [
        to(upper, relay.at[2:4], v.at[2:4, mid], hop, 2),
        to(upper, relay.at[0:2], v.at[0:2, mid], hop, 3),
    ]
    hop_south = [
        to(first, v_hbm.at[4:6, mid], relay.at[0:2], hop, 4),
        to(first, v_hbm.at[6:7, mid], relay.at[2:3], hop, 5),
    ]
    on_south = [
        to(lower, relay.at[0:2], v.at[FAR + 4:FAR + 6, mid], hop, 6),
        to(lower, relay.at[2:3], v.at[FAR + 6:FAR + 7, mid], hop, 7),
    ]

    @pl.when(below)
    def _():
        for copy in hop_north:
            copy.start()

    @pl.when(above)
    def _():
        for copy in hop_south:
            copy.start()

    @pl.when(has_north)
    def _():
        for copy in northward:
            copy.start()

    @pl.when(has_south)
    def _():
        for copy in southward:
            copy.start()

    @pl.when(jnp.logical_and(has_north, jnp.logical_not(below)))
    def _():
        north_far.start()

    @pl.when(jnp.logical_and(has_south, jnp.logical_not(above)))
    def _():
        south_far.start()

    v[EXT - 1] = jnp.zeros((NCOLS, FIELDS), f32)

    @pl.when(at_first)
    def _():
        v[0:HALO] = jnp.zeros((HALO, NCOLS, FIELDS), f32)
        w[0:HALO] = jnp.zeros((HALO, 16, NCOLS), f32)
        da[0:HALO] = jnp.zeros((HALO, NCOLS), i32)
        db[0:HALO] = jnp.zeros((HALO, NCOLS), i32)

    @pl.when(at_last)
    def _():
        v[FAR:EXT - 1] = jnp.zeros((HALO - 1, NCOLS, FIELDS), f32)
        w[FAR:EXT] = jnp.zeros((HALO, 16, NCOLS), f32)
        da[FAR:EXT] = jnp.zeros((HALO, NCOLS), i32)
        db[FAR:EXT] = jnp.zeros((HALO, NCOLS), i32)

    acc[...] = jnp.zeros_like(acc)
    side[...] = jnp.zeros_like(side)
    for copy in own:
        copy.wait()

    lane = lax.broadcasted_iota(i32, (1, KEYS), 1)

    def split(values):
        high = values.astype(bf16)
        return high, (values - high.astype(f32)).astype(bf16)

    def multiply(total, start, size, width, values):
        rhs[0:KEYS], rhs[KEYS:2 * KEYS] = split(values)
        tall = slice(0, size * width)
        for n in range(FIELDS // HALF):
            part = slice(n * HALF, (n + 1) * HALF)
            c = jnp.concatenate([coef[tall, 0:KEYS], coef[tall, KEYS:2 * KEYS], coef[tall, 0:KEYS]], axis=1)
            r = jnp.concatenate([rhs[0:KEYS, part], rhs[0:KEYS, part], rhs[KEYS:2 * KEYS, part]], axis=0)
            out = jnp.dot(c, r, preferred_element_type=f32)
            total[pl.ds(start, size), :, part] += out.reshape(size, width, HALF)

    def place_rows(base, size, width, highs, lows):
        for t in range(size):
            pick = [jnp.broadcast_to((base == t - a).astype(f32), (16, KEYS)).astype(bf16) for a in range(4)]
            pick = [jnp.concatenate([p] * (width // 16), axis=0) for p in pick]
            place = slice(t * width, (t + 1) * width)
            coef[place, 0:KEYS] = sum(p * g for p, g in zip(pick, highs))
            coef[place, KEYS:2 * KEYS] = sum(p * g for p, g in zip(pick, lows))

    def deposit(source, start, size):
        def rows(ref):
            return jnp.concatenate([ref[pl.ds(source + k, 1), :] for k in range(GROUP)], axis=1)
        weights = jnp.concatenate([w[source + k] for k in range(GROUP)], axis=1)
        column = lax.broadcasted_iota(i32, (NCOLS, KEYS), 0) - (lane % NCOLS + rows(db) - 1)
        at = [column == b for b in range(4)]
        highs, lows = [], []
        for a in range(4):
            g = jnp.zeros((NCOLS, KEYS), f32)
            for b in range(4):
                g = jnp.where(at[b], weights[4 * a + b:4 * a + b + 1], g)
            h, low = split(g)
            highs.append(h)
            lows.append(low)
        base = lane // NCOLS + rows(da) + (source - HALO - 1) - start
        place_rows(base, size, NCOLS, highs, lows)
        multiply(acc, start, size, NCOLS, v[pl.ds(source, GROUP)].reshape(KEYS, FIELDS))

    def deposit_sides(source, start, size):
        many = EDGE_GROUP * NCOLS

        def rows(ref):
            joined = jnp.concatenate([ref[source + k:source + k + 1, :] for k in range(EDGE_GROUP)], axis=1)
            return jnp.broadcast_to(joined.astype(f32), (16, many)).astype(bf16)
        high, low = split(jnp.concatenate([w[source + k] for k in range(EDGE_GROUP)], axis=1))
        stacked = jnp.concatenate([high, low, rows(da), rows(db)], axis=0)
        row_of, col_of = lane % 128 // 8, lane % 8 + (NCOLS - HALO) * (lane // 128)
        chosen = (lax.broadcasted_iota(i32, (many, KEYS), 0) == row_of * NCOLS + col_of).astype(f32).astype(bf16)
        packed = jnp.dot(stacked, chosen, preferred_element_type=f32)
        step_a, step_b = packed[32:33].astype(i32), packed[48:49].astype(i32)
        target = lax.broadcasted_iota(i32, (16, KEYS), 0)
        target = jnp.where(target < HALO, target - HALO, target + (NCOLS - HALO))
        column = target - (col_of + step_b - 1)
        at = [column == b for b in range(4)]
        kept = []
        for part in (0, 16):
            for a in range(4):
                g = jnp.zeros((16, KEYS), f32)
                for b in range(4):
                    g = jnp.where(at[b], packed[part + 4 * a + b:part + 4 * a + b + 1], g)
                kept.append(g.astype(bf16))
        base = row_of + step_a + (source - HALO - 1) - start
        place_rows(base, size, 16, kept[:4], kept[4:])
        near = slice(source, source + EDGE_GROUP)
        values = jnp.concatenate(
            [v[near, left].reshape(KEYS // 2, FIELDS), v[near, right].reshape(KEYS // 2, FIELDS)], axis=0)
        multiply(side, start, size, 16, values)

    deposit_sides(HALO + 8, 1, 31)

    @pl.loop(0, 4)
    def _(k):
        deposit(HALO + 8 + 4 * k, 1 + 4 * k, 19)

    @pl.when(at_last)
    def _():
        for here, onward in zip(hop_north, on_north):
            here.wait_recv()
            onward.start()

    @pl.when(at_first)
    def _():
        for here, onward in zip(hop_south, on_south):
            here.wait_recv()
            onward.start()

    @pl.when(has_south)
    def _():
        for copy in northward[:5]:
            copy.wait_recv()

    @pl.when(has_north)
    def _():
        for copy in southward[:5]:
            copy.wait_recv()

    deposit_sides(0, 0, 16)
    deposit_sides(HALO + 24, 17, 15)
    sideward = [
        to(west, side.at[:, 0:HALO], side_in.at[1], lon, 0),
        to(east, side.at[:, HALO:2 * HALO], side_in.at[0], lon, 1),
    ]
    for copy in sideward:
        copy.start()

    @pl.loop(0, 2)
    def _(k):
        deposit(HALO + 4 + 20 * k, 16 * k, 16)

    @pl.loop(0, 2)
    def _(k):
        deposit(HALO + 28 * k, 20 * k, 12)

    for copy in sideward:
        copy.wait_recv()
    acc[:, left] += side_in[0]
    acc[:, right] += side_in[1]

    def write(source, count, k):
        copy = pltpu.make_async_copy(
            acc.at[source:source + count], out_hbm.at[source:source + count], out_sem.at[k])
        copy.start()
        return copy

    written = [write(8, 16, 0)]

    @pl.when(has_south)
    def _():
        northward[5].wait_recv()

    @pl.when(has_north)
    def _():
        southward[5].wait_recv()

    def one_has(k):
        return jnp.logical_or(jnp.logical_and(k == 0, has_south), jnp.logical_and(k == 1, has_north))

    @pl.loop(0, 2)
    def _(k):
        @pl.when(one_has(k))
        def _():
            deposit(4 + (FAR - 4) * k, 24 * k, 8)

    written += [write(4, 4, 1), write(24, 4, 2)]

    @pl.when(jnp.logical_and(has_south, jnp.logical_not(above)))
    def _():
        north_far.wait_recv()

    @pl.when(above)
    def _():
        for copy in on_north:
            copy.wait_recv()

    @pl.when(jnp.logical_and(has_north, jnp.logical_not(below)))
    def _():
        south_far.wait_recv()

    @pl.when(below)
    def _():
        for copy in on_south:
            copy.wait_recv()

    @pl.loop(0, 2)
    def _(k):
        @pl.when(one_has(k))
        def _():
            deposit((FAR + 4) * k, 28 * k, 4)

    written += [write(0, 4, 3), write(28, 4, 4)]

    @pl.when(has_north)
    def _():
        for copy in northward:
            copy.wait_send()

    @pl.when(has_south)
    def _():
        for copy in southward:
            copy.wait_send()

    @pl.when(jnp.logical_and(has_north, jnp.logical_not(below)))
    def _():
        north_far.wait_send()

    @pl.when(jnp.logical_and(has_south, jnp.logical_not(above)))
    def _():
        south_far.wait_send()

    @pl.when(below)
    def _():
        for copy in hop_north:
            copy.wait_send()

    @pl.when(above)
    def _():
        for copy in hop_south:
            copy.wait_send()

    @pl.when(at_last)
    def _():
        for copy in on_north:
            copy.wait_send()

    @pl.when(at_first)
    def _():
        for copy in on_south:
            copy.wait_send()

    for copy in sideward:
        copy.wait_send()
    for copy in written:
        copy.wait()


def body(adj_arrival, weights, dep_lat, dep_lon):
    by_point = jnp.transpose(weights, (0, 2, 1))
    hbm = pl.BlockSpec(memory_space=pl.ANY)
    dma = pltpu.SemaphoreType.DMA
    return pl.pallas_call(
        kernel,
        out_shape=jax.ShapeDtypeStruct((NROWS, NCOLS, FIELDS), f32),
        in_specs=[hbm] * 4,
        out_specs=hbm,
        scratch_shapes=[
            pltpu.VMEM((EXT, NCOLS, FIELDS), f32),
            pltpu.VMEM((EXT, 16, NCOLS), f32),
            pltpu.VMEM((EXT, NCOLS), i32),
            pltpu.VMEM((EXT, NCOLS), i32),
            pltpu.VMEM((NROWS, NCOLS, FIELDS), f32),
            pltpu.VMEM((NROWS, 2 * HALO, FIELDS), f32),
            pltpu.VMEM((2, NROWS, HALO, FIELDS), f32),
            pltpu.VMEM((GROUP, NCOLS - 2 * HALO, FIELDS), f32),
            pltpu.VMEM((19 * NCOLS, 2 * KEYS), bf16),
            pltpu.VMEM((2 * KEYS, FIELDS), bf16),
            dma((14,)), dma((14,)), dma((8,)), dma((8,)), dma((2,)), dma((2,)), dma((4,)), dma((5,)),
        ],
        compiler_params=pltpu.CompilerParams(
            collective_id=0, has_side_effects=True, vmem_limit_bytes=24 << 20),
    )(*(pltpu.with_memory_space_constraint(x, pltpu.HBM) for x in (adj_arrival, by_point, dep_lat, dep_lon)))


def solution(mesh):
    placed = (P("lat", "lon", None), P("lat", "lon", None), P("lat", "lon"), P("lat", "lon"))
    return jax.shard_map(
        body, mesh=mesh, in_specs=placed, out_specs=P("lat", "lon", None), check_vma=False
    )
```

```python
import jax
import jax.numpy as jnp
from jax import lax
from jax.experimental import pallas as pl
from jax.experimental.pallas import tpu as pltpu
from jax.sharding import PartitionSpec as P

NROWS, NCOLS, FIELDS = 32, 64, 512
HALO = 8
FAR = HALO + NROWS
EXT = FAR + HALO
GROUP = 4
KEYS = GROUP * NCOLS
EDGE_GROUP = 16
HALF = 256
MESH = pl.DeviceIdType.MESH
f32, bf16, i32 = jnp.float32, jnp.bfloat16, jnp.int32


def kernel(v_hbm, w_hbm, da_hbm, db_hbm, out_hbm,
           v, w, packs, pack_in, da, db, acc, side, side_in, relay, coef, rhs,
           lat_send, lat_recv, hop_send, hop_recv, lon_send, lon_recv, own_sem, out_sem):
    nlat, nlon = lax.axis_size("lat"), lax.axis_size("lon")
    half_lat = nlat // 2
    la, lo = lax.axis_index("lat"), lax.axis_index("lon")
    has_south, has_north = la > 0, la < nlat - 1
    at_first, at_last = la == 0, la == nlat - 1
    below, above = la == half_lat - 1, la == half_lat
    at_end, at_middle = jnp.logical_or(at_first, at_last), jnp.logical_or(below, above)
    south, north = {"lat": jnp.maximum(la - 1, 0)}, {"lat": jnp.minimum(la + 1, nlat - 1)}
    east, west = {"lon": lax.rem(lo + 1, nlon)}, {"lon": lax.rem(lo + nlon - 1, nlon)}
    first, last = {"lat": jnp.int32(0)}, {"lat": jnp.int32(nlat - 1)}
    lower, upper = {"lat": jnp.int32(half_lat - 1)}, {"lat": jnp.int32(half_lat)}

    barrier = pltpu.get_barrier_semaphore()

    def greet(device):
        pl.semaphore_signal(barrier, inc=1, device_id=device, device_id_type=MESH)

    greet(east)
    greet(west)

    @pl.when(has_north)
    def _():
        greet(north)

    @pl.when(has_south)
    def _():
        greet(south)

    @pl.when(at_end)
    def _():
        greet(lower)
        greet(upper)

    @pl.when(at_middle)
    def _():
        greet(first)
        greet(last)

    own = [
        pltpu.make_async_copy(v_hbm, v.at[HALO:FAR], own_sem.at[0]),
        pltpu.make_async_copy(w_hbm, w.at[HALO:FAR], own_sem.at[1]),
        pltpu.make_async_copy(da_hbm, da.at[HALO:FAR], own_sem.at[2]),
        pltpu.make_async_copy(db_hbm, db.at[HALO:FAR], own_sem.at[3]),
    ]
    for copy in own:
        copy.start()
    pl.semaphore_wait(
        barrier,
        2 + has_north.astype(i32) + has_south.astype(i32) + 2 * at_end.astype(i32) + 2 * at_middle.astype(i32))

    def to(device, src, dst, sems, k):
        return pltpu.make_async_remote_copy(
            src_ref=src, dst_ref=dst, send_sem=sems[0].at[k], recv_sem=sems[1].at[k],
            device_id=device, device_id_type=MESH)

    lat, hop, lon = (lat_send, lat_recv), (hop_send, hop_recv), (lon_send, lon_recv)
    mid = slice(HALO, NCOLS - HALO)
    left, right = slice(0, HALO), slice(NCOLS - HALO, NCOLS)
    northward = [
        to(north, v_hbm.at[24:32, left], v.at[0:8, left], lat, 0),
        to(north, v_hbm.at[24:32, right], v.at[0:8, right], lat, 1),
        to(north, packs.at[0], pack_in.at[0], lat, 2),
        to(north, da_hbm.at[24:32], da.at[0:8], lat, 3),
        to(north, db_hbm.at[24:32], db.at[0:8], lat, 4),
        to(north, v_hbm.at[28:32, mid], v.at[4:8, mid], lat, 5),
    ]
    north_far = to(north, v_hbm.at[24:28, mid], v.at[0:4, mid], lat, 6)
    southward = [
        to(south, v_hbm.at[0:7, left], v.at[FAR:FAR + 7, left], lat, 7),
        to(south, v_hbm.at[0:7, right], v.at[FAR:FAR + 7, right], lat, 8),
        to(south, packs.at[1], pack_in.at[1], lat, 9),
        to(south, da_hbm.at[0:8], da.at[FAR:FAR + 8], lat, 10),
        to(south, db_hbm.at[0:8], db.at[FAR:FAR + 8], lat, 11),
        to(south, v_hbm.at[0:4, mid], v.at[FAR:FAR + 4, mid], lat, 12),
    ]
    south_far = to(south, v_hbm.at[4:7, mid], v.at[FAR + 4:FAR + 7, mid], lat, 13)
    hop_north = [
        to(last, v_hbm.at[26:28, mid], relay.at[2:4], hop, 0),
        to(last, v_hbm.at[24:26, mid], relay.at[0:2], hop, 1),
    ]
    on_north = [
        to(upper, relay.at[2:4], v.at[2:4, mid], hop, 2),
        to(upper, relay.at[0:2], v.at[0:2, mid], hop, 3),
    ]
    hop_south = [
        to(first, v_hbm.at[4:6, mid], relay.at[0:2], hop, 4),
        to(first, v_hbm.at[6:7, mid], relay.at[2:3], hop, 5),
    ]
    on_south = [
        to(lower, relay.at[0:2], v.at[FAR + 4:FAR + 6, mid], hop, 6),
        to(lower, relay.at[2:3], v.at[FAR + 6:FAR + 7, mid], hop, 7),
    ]

    @pl.when(below)
    def _():
        for copy in hop_north:
            copy.start()

    @pl.when(above)
    def _():
        for copy in hop_south:
            copy.start()

    @pl.when(has_north)
    def _():
        for copy in northward[:2]:
            copy.start()

    @pl.when(has_south)
    def _():
        for copy in southward[:2]:
            copy.start()

    own[1].wait()
    for m in range(HALO // 2):
        for p, source in ((0, FAR - HALO), (1, HALO)):
            packs[p, m] = jnp.concatenate([w[source + 2 * m], w[source + 2 * m + 1]], axis=1)

    @pl.when(has_north)
    def _():
        for copy in northward[2:]:
            copy.start()

    @pl.when(has_south)
    def _():
        for copy in southward[2:]:
            copy.start()

    @pl.when(jnp.logical_and(has_north, jnp.logical_not(below)))
    def _():
        north_far.start()

    @pl.when(jnp.logical_and(has_south, jnp.logical_not(above)))
    def _():
        south_far.start()

    v[EXT - 1] = jnp.zeros((NCOLS, FIELDS), f32)

    @pl.when(at_first)
    def _():
        v[0:HALO] = jnp.zeros((HALO, NCOLS, FIELDS), f32)
        pack_in[0] = jnp.zeros((HALO // 2, 16, 2 * NCOLS), f32)
        da[0:HALO] = jnp.zeros((HALO, NCOLS), i32)
        db[0:HALO] = jnp.zeros((HALO, NCOLS), i32)

    @pl.when(at_last)
    def _():
        v[FAR:EXT - 1] = jnp.zeros((HALO - 1, NCOLS, FIELDS), f32)
        pack_in[1] = jnp.zeros((HALO // 2, 16, 2 * NCOLS), f32)
        da[FAR:EXT] = jnp.zeros((HALO, NCOLS), i32)
        db[FAR:EXT] = jnp.zeros((HALO, NCOLS), i32)

    acc[...] = jnp.zeros_like(acc)
    side[...] = jnp.zeros_like(side)
    for copy in own[:1] + own[2:]:
        copy.wait()

    lane = lax.broadcasted_iota(i32, (1, KEYS), 1)

    def split(values):
        high = values.astype(bf16)
        return high, (values - high.astype(f32)).astype(bf16)

    def multiply(total, start, size, width, values):
        rhs[0:KEYS], rhs[KEYS:2 * KEYS] = split(values)
        tall = slice(0, size * width)
        for n in range(FIELDS // HALF):
            part = slice(n * HALF, (n + 1) * HALF)
            c = jnp.concatenate([coef[tall, 0:KEYS], coef[tall, KEYS:2 * KEYS], coef[tall, 0:KEYS]], axis=1)
            r = jnp.concatenate([rhs[0:KEYS, part], rhs[0:KEYS, part], rhs[KEYS:2 * KEYS, part]], axis=0)
            out = jnp.dot(c, r, preferred_element_type=f32)
            total[pl.ds(start, size), :, part] += out.reshape(size, width, HALF)

    def place_rows(base, size, width, highs, lows):
        for t in range(size):
            pick = [jnp.broadcast_to((base == t - a).astype(f32), (16, KEYS)).astype(bf16) for a in range(4)]
            pick = [jnp.concatenate([p] * (width // 16), axis=0) for p in pick]
            place = slice(t * width, (t + 1) * width)
            coef[place, 0:KEYS] = sum(p * g for p, g in zip(pick, highs))
            coef[place, KEYS:2 * KEYS] = sum(p * g for p, g in zip(pick, lows))

    def deposit(source, start, size):
        def rows(ref):
            return jnp.concatenate([ref[pl.ds(source + k, 1), :] for k in range(GROUP)], axis=1)
        weights = jnp.concatenate([w[source + k] for k in range(GROUP)], axis=1)
        column = lax.broadcasted_iota(i32, (NCOLS, KEYS), 0) - (lane % NCOLS + rows(db) - 1)
        at = [column == b for b in range(4)]
        highs, lows = [], []
        for a in range(4):
            g = jnp.zeros((NCOLS, KEYS), f32)
            for b in range(4):
                g = jnp.where(at[b], weights[4 * a + b:4 * a + b + 1], g)
            h, low = split(g)
            highs.append(h)
            lows.append(low)
        base = lane // NCOLS + rows(da) + (source - HALO - 1) - start
        place_rows(base, size, NCOLS, highs, lows)
        multiply(acc, start, size, NCOLS, v[pl.ds(source, GROUP)].reshape(KEYS, FIELDS))

    def deposit_sides(sources, *spans):
        many = EDGE_GROUP * NCOLS

        def rows(ref):
            joined = jnp.concatenate([ref[r:r + 1, :] for r in sources], axis=1)
            return jnp.broadcast_to(joined.astype(f32), (16, many)).astype(bf16)
        high, low = split(jnp.concatenate([w[r] for r in sources], axis=1))
        stacked = jnp.concatenate([high, low, rows(da), rows(db)], axis=0)
        row_of, col_of = lane % 128 // 8, lane % 8 + (NCOLS - HALO) * (lane // 128)
        chosen = (lax.broadcasted_iota(i32, (many, KEYS), 0) == row_of * NCOLS + col_of).astype(f32).astype(bf16)
        packed = jnp.dot(stacked, chosen, preferred_element_type=f32)
        step_a, step_b = packed[32:33].astype(i32), packed[48:49].astype(i32)
        target = lax.broadcasted_iota(i32, (16, KEYS), 0)
        target = jnp.where(target < HALO, target - HALO, target + (NCOLS - HALO))
        column = target - (col_of + step_b - 1)
        at = [column == b for b in range(4)]
        kept = []
        for part in (0, 16):
            for a in range(4):
                g = jnp.zeros((16, KEYS), f32)
                for b in range(4):
                    g = jnp.where(at[b], packed[part + 4 * a + b:part + 4 * a + b + 1], g)
                kept.append(g.astype(bf16))
        values = jnp.concatenate(
            [v[r:r + HALO, columns].reshape(KEYS // 4, FIELDS)
             for columns in (left, right) for r in (sources[0], sources[HALO])], axis=0)
        source = jnp.where(row_of < HALO, row_of + sources[0], row_of + (sources[HALO] - HALO))
        for start, size in spans:
            place_rows(source + step_a - (HALO + 1) - start, size, 16, kept[:4], kept[4:])
            multiply(side, start, size, 16, values)

    def sides(start, size, k):
        return [
            to(west, side.at[start:start + size, 0:HALO], side_in.at[1, start:start + size], lon, k),
            to(east, side.at[start:start + size, HALO:2 * HALO], side_in.at[0, start:start + size], lon, k + 1),
        ]

    deposit_sides([HALO + k for k in range(16)], (0, 24))
    deposit_sides([HALO + 16 + k for k in range(16)], (9, 23))
    sideward = sides(8, 16, 0)
    for copy in sideward:
        copy.start()

    @pl.loop(0, 4)
    def _(k):
        deposit(HALO + 8 + 4 * k, 1 + 4 * k, 19)

        @pl.when(jnp.logical_and(k == 2, at_last))
        def _():
            for here, onward in zip(hop_north, on_north):
                here.wait_recv()
                onward.start()

        @pl.when(jnp.logical_and(k == 2, at_first))
        def _():
            for here, onward in zip(hop_south, on_south):
                here.wait_recv()
                onward.start()

    @pl.when(has_south)
    def _():
        for copy in northward[:5]:
            copy.wait_recv()

    @pl.when(has_north)
    def _():
        for copy in southward[:5]:
            copy.wait_recv()

    for m in range(HALO // 2):
        for p, source in ((0, 0), (1, FAR)):
            pair = pack_in[p, m]
            w[source + 2 * m] = pair[:, 0:NCOLS]
            w[source + 2 * m + 1] = pair[:, NCOLS:2 * NCOLS]
    deposit_sides([k for k in range(8)] + [FAR + k for k in range(8)], (0, 8), (24, 8))
    ends = sides(0, 8, 2) + sides(24, 8, 4)
    for copy in ends:
        copy.start()
    sideward += ends

    @pl.loop(0, 2)
    def _(k):
        deposit(HALO + 4 + 20 * k, 16 * k, 16)

    @pl.loop(0, 2)
    def _(k):
        deposit(HALO + 28 * k, 20 * k, 12)

    written = []

    def write(rows, columns):
        copy = pltpu.make_async_copy(acc.at[rows, columns], out_hbm.at[rows, columns], out_sem.at[len(written)])
        copy.start()
        written.append(copy)

    @pl.when(has_north)
    def _():
        southward[5].wait_recv()
        deposit(FAR, 24, 8)

    @pl.when(has_south)
    def _():
        northward[5].wait_recv()
        deposit(4, 0, 8)

    write(slice(4, 28), mid)

    @pl.when(jnp.logical_and(has_north, jnp.logical_not(below)))
    def _():
        south_far.wait_recv()

    @pl.when(below)
    def _():
        for copy in on_south:
            copy.wait_recv()

    @pl.when(has_north)
    def _():
        deposit(FAR + 4, 28, 4)

    write(slice(28, 32), mid)
    for copy in sideward:
        copy.wait_recv()
    acc[:, left] += side_in[0]
    acc[:, right] += side_in[1]
    for columns in (left, right):
        write(slice(4, 32), columns)

    @pl.when(jnp.logical_and(has_south, jnp.logical_not(above)))
    def _():
        north_far.wait_recv()

    @pl.when(above)
    def _():
        for copy in on_north:
            copy.wait_recv()

    @pl.when(has_south)
    def _():
        deposit(0, 0, 4)

    write(slice(0, 4), slice(0, NCOLS))

    @pl.when(has_north)
    def _():
        for copy in northward:
            copy.wait_send()

    @pl.when(has_south)
    def _():
        for copy in southward:
            copy.wait_send()

    @pl.when(jnp.logical_and(has_north, jnp.logical_not(below)))
    def _():
        north_far.wait_send()

    @pl.when(jnp.logical_and(has_south, jnp.logical_not(above)))
    def _():
        south_far.wait_send()

    @pl.when(below)
    def _():
        for copy in hop_north:
            copy.wait_send()

    @pl.when(above)
    def _():
        for copy in hop_south:
            copy.wait_send()

    @pl.when(at_last)
    def _():
        for copy in on_north:
            copy.wait_send()

    @pl.when(at_first)
    def _():
        for copy in on_south:
            copy.wait_send()

    for copy in sideward:
        copy.wait_send()
    for copy in written:
        copy.wait()


def body(adj_arrival, weights, dep_lat, dep_lon):
    by_point = jnp.transpose(weights, (0, 2, 1))
    hbm = pl.BlockSpec(memory_space=pl.ANY)
    dma = pltpu.SemaphoreType.DMA
    return pl.pallas_call(
        kernel,
        out_shape=jax.ShapeDtypeStruct((NROWS, NCOLS, FIELDS), f32),
        in_specs=[hbm] * 4,
        out_specs=hbm,
        scratch_shapes=[
            pltpu.VMEM((EXT, NCOLS, FIELDS), f32),
            pltpu.VMEM((EXT, 16, NCOLS), f32),
            pltpu.VMEM((2, HALO // 2, 16, 2 * NCOLS), f32),
            pltpu.VMEM((2, HALO // 2, 16, 2 * NCOLS), f32),
            pltpu.VMEM((EXT, NCOLS), i32),
            pltpu.VMEM((EXT, NCOLS), i32),
            pltpu.VMEM((NROWS, NCOLS, FIELDS), f32),
            pltpu.VMEM((NROWS, 2 * HALO, FIELDS), f32),
            pltpu.VMEM((2, NROWS, HALO, FIELDS), f32),
            pltpu.VMEM((GROUP, NCOLS - 2 * HALO, FIELDS), f32),
            pltpu.VMEM((19 * NCOLS, 2 * KEYS), bf16),
            pltpu.VMEM((2 * KEYS, FIELDS), bf16),
            dma((14,)), dma((14,)), dma((8,)), dma((8,)), dma((6,)), dma((6,)), dma((4,)), dma((5,)),
        ],
        compiler_params=pltpu.CompilerParams(
            collective_id=0, has_side_effects=True, vmem_limit_bytes=24 << 20),
    )(*(pltpu.with_memory_space_constraint(x, pltpu.HBM) for x in (adj_arrival, by_point, dep_lat, dep_lon)))


def solution(mesh):
    placed = (P("lat", "lon", None), P("lat", "lon", None), P("lat", "lon"), P("lat", "lon"))
    return jax.shard_map(
        body, mesh=mesh, in_specs=placed, out_specs=P("lat", "lon", None), check_vma=False
    )
```

```python
import jax
import jax.numpy as jnp
from jax import lax
from jax.experimental import pallas as pl
from jax.experimental.pallas import tpu as pltpu
from jax.sharding import PartitionSpec as P

NROWS, NCOLS, FIELDS = 32, 64, 512
HALO = 8
FAR = HALO + NROWS
EXT = FAR + HALO
GROUP = 4
KEYS = GROUP * NCOLS
EDGE_GROUP = 16
HALF = 256
MESH = pl.DeviceIdType.MESH
f32, bf16, i32 = jnp.float32, jnp.bfloat16, jnp.int32


def kernel(v_hbm, w_hbm, da_hbm, db_hbm, out_hbm, far_out, coef_out,
           v, w, packs, pack_in, da, db, acc, side, side_in, relay, coef, last_coef, rhs,
           lat_send, lat_recv, hop_send, hop_recv, lon_send, lon_recv, own_sem, out_sem, hand_sem):
    nlat, nlon = lax.axis_size("lat"), lax.axis_size("lon")
    half_lat = nlat // 2
    la, lo = lax.axis_index("lat"), lax.axis_index("lon")
    has_south, has_north = la > 0, la < nlat - 1
    at_first, at_last = la == 0, la == nlat - 1
    below, above = la == half_lat - 1, la == half_lat
    at_end, at_middle = jnp.logical_or(at_first, at_last), jnp.logical_or(below, above)
    south, north = {"lat": jnp.maximum(la - 1, 0)}, {"lat": jnp.minimum(la + 1, nlat - 1)}
    east, west = {"lon": lax.rem(lo + 1, nlon)}, {"lon": lax.rem(lo + nlon - 1, nlon)}
    first, last = {"lat": jnp.int32(0)}, {"lat": jnp.int32(nlat - 1)}
    lower, upper = {"lat": jnp.int32(half_lat - 1)}, {"lat": jnp.int32(half_lat)}

    barrier = pltpu.get_barrier_semaphore()

    def greet(device):
        pl.semaphore_signal(barrier, inc=1, device_id=device, device_id_type=MESH)

    greet(east)
    greet(west)

    @pl.when(has_north)
    def _():
        greet(north)

    @pl.when(has_south)
    def _():
        greet(south)

    @pl.when(at_end)
    def _():
        greet(lower)
        greet(upper)

    @pl.when(at_middle)
    def _():
        greet(first)
        greet(last)

    own = [
        pltpu.make_async_copy(v_hbm, v.at[HALO:FAR], own_sem.at[0]),
        pltpu.make_async_copy(w_hbm, w.at[HALO:FAR], own_sem.at[1]),
        pltpu.make_async_copy(da_hbm, da.at[HALO:FAR], own_sem.at[2]),
        pltpu.make_async_copy(db_hbm, db.at[HALO:FAR], own_sem.at[3]),
    ]
    for copy in own:
        copy.start()
    pl.semaphore_wait(
        barrier,
        2 + has_north.astype(i32) + has_south.astype(i32) + 2 * at_end.astype(i32) + 2 * at_middle.astype(i32))

    def to(device, src, dst, sems, k):
        return pltpu.make_async_remote_copy(
            src_ref=src, dst_ref=dst, send_sem=sems[0].at[k], recv_sem=sems[1].at[k],
            device_id=device, device_id_type=MESH)

    lat, hop, lon = (lat_send, lat_recv), (hop_send, hop_recv), (lon_send, lon_recv)
    mid = slice(HALO, NCOLS - HALO)
    left, right = slice(0, HALO), slice(NCOLS - HALO, NCOLS)
    northward = [
        to(north, v_hbm.at[24:32, left], v.at[0:8, left], lat, 0),
        to(north, v_hbm.at[24:32, right], v.at[0:8, right], lat, 1),
        to(north, packs.at[0], pack_in.at[0], lat, 2),
        to(north, da_hbm.at[24:32], da.at[0:8], lat, 3),
        to(north, db_hbm.at[24:32], db.at[0:8], lat, 4),
        to(north, v_hbm.at[28:32, mid], v.at[4:8, mid], lat, 5),
    ]
    north_far = to(north, v_hbm.at[24:28, mid], far_out.at[:, mid], lat, 6)
    southward = [
        to(south, v_hbm.at[0:7, left], v.at[FAR:FAR + 7, left], lat, 7),
        to(south, v_hbm.at[0:7, right], v.at[FAR:FAR + 7, right], lat, 8),
        to(south, packs.at[1], pack_in.at[1], lat, 9),
        to(south, da_hbm.at[0:8], da.at[FAR:FAR + 8], lat, 10),
        to(south, db_hbm.at[0:8], db.at[FAR:FAR + 8], lat, 11),
        to(south, v_hbm.at[0:4, mid], v.at[FAR:FAR + 4, mid], lat, 12),
    ]
    south_far = to(south, v_hbm.at[4:7, mid], v.at[FAR + 4:FAR + 7, mid], lat, 13)
    hop_north = [
        to(last, v_hbm.at[26:28, mid], relay.at[2:4], hop, 0),
        to(last, v_hbm.at[24:26, mid], relay.at[0:2], hop, 1),
    ]
    on_north = [
        to(upper, relay.at[2:4], far_out.at[2:4, mid], hop, 2),
        to(upper, relay.at[0:2], far_out.at[0:2, mid], hop, 3),
    ]
    hop_south = [
        to(first, v_hbm.at[4:6, mid], relay.at[0:2], hop, 4),
        to(first, v_hbm.at[6:7, mid], relay.at[2:3], hop, 5),
    ]
    on_south = [
        to(lower, relay.at[0:2], v.at[FAR + 4:FAR + 6, mid], hop, 6),
        to(lower, relay.at[2:3], v.at[FAR + 6:FAR + 7, mid], hop, 7),
    ]

    @pl.when(below)
    def _():
        for copy in hop_north:
            copy.start()

    @pl.when(above)
    def _():
        for copy in hop_south:
            copy.start()

    @pl.when(has_north)
    def _():
        for copy in northward[:2]:
            copy.start()

    @pl.when(has_south)
    def _():
        for copy in southward[:2]:
            copy.start()

    own[1].wait()
    for m in range(HALO // 2):
        for p, source in ((0, FAR - HALO), (1, HALO)):
            packs[p, m] = jnp.concatenate([w[source + 2 * m], w[source + 2 * m + 1]], axis=1)

    @pl.when(has_north)
    def _():
        for copy in northward[2:]:
            copy.start()

    @pl.when(has_south)
    def _():
        for copy in southward[2:]:
            copy.start()

    @pl.when(jnp.logical_and(has_north, jnp.logical_not(below)))
    def _():
        north_far.start()

    @pl.when(jnp.logical_and(has_south, jnp.logical_not(above)))
    def _():
        south_far.start()

    v[EXT - 1] = jnp.zeros((NCOLS, FIELDS), f32)

    @pl.when(at_first)
    def _():
        v[0:HALO] = jnp.zeros((HALO, NCOLS, FIELDS), f32)
        pack_in[0] = jnp.zeros((HALO // 2, 16, 2 * NCOLS), f32)
        da[0:HALO] = jnp.zeros((HALO, NCOLS), i32)
        db[0:HALO] = jnp.zeros((HALO, NCOLS), i32)

    @pl.when(at_last)
    def _():
        v[FAR:EXT - 1] = jnp.zeros((HALO - 1, NCOLS, FIELDS), f32)
        pack_in[1] = jnp.zeros((HALO // 2, 16, 2 * NCOLS), f32)
        da[FAR:EXT] = jnp.zeros((HALO, NCOLS), i32)
        db[FAR:EXT] = jnp.zeros((HALO, NCOLS), i32)

    acc[...] = jnp.zeros_like(acc)
    side[...] = jnp.zeros_like(side)
    for copy in own[:1] + own[2:]:
        copy.wait()

    lane = lax.broadcasted_iota(i32, (1, KEYS), 1)

    def split(values):
        high = values.astype(bf16)
        return high, (values - high.astype(f32)).astype(bf16)

    def multiply(total, start, size, width, values):
        rhs[0:KEYS], rhs[KEYS:2 * KEYS] = split(values)
        tall = slice(0, size * width)
        for n in range(FIELDS // HALF):
            part = slice(n * HALF, (n + 1) * HALF)
            c = jnp.concatenate([coef[tall, 0:KEYS], coef[tall, KEYS:2 * KEYS], coef[tall, 0:KEYS]], axis=1)
            r = jnp.concatenate([rhs[0:KEYS, part], rhs[0:KEYS, part], rhs[KEYS:2 * KEYS, part]], axis=0)
            out = jnp.dot(c, r, preferred_element_type=f32)
            total[pl.ds(start, size), :, part] += out.reshape(size, width, HALF)

    def place_rows(into, base, size, width, highs, lows):
        for t in range(size):
            pick = [jnp.broadcast_to((base == t - a).astype(f32), (16, KEYS)).astype(bf16) for a in range(4)]
            pick = [jnp.concatenate([p] * (width // 16), axis=0) for p in pick]
            place = slice(t * width, (t + 1) * width)
            into[place, 0:KEYS] = sum(p * g for p, g in zip(pick, highs))
            into[place, KEYS:2 * KEYS] = sum(p * g for p, g in zip(pick, lows))

    def prepare(into, source, start, size):
        def rows(ref):
            return jnp.concatenate([ref[pl.ds(source + k, 1), :] for k in range(GROUP)], axis=1)
        weights = jnp.concatenate([w[source + k] for k in range(GROUP)], axis=1)
        column = lax.broadcasted_iota(i32, (NCOLS, KEYS), 0) - (lane % NCOLS + rows(db) - 1)
        at = [column == b for b in range(4)]
        highs, lows = [], []
        for a in range(4):
            g = jnp.zeros((NCOLS, KEYS), f32)
            for b in range(4):
                g = jnp.where(at[b], weights[4 * a + b:4 * a + b + 1], g)
            h, low = split(g)
            highs.append(h)
            lows.append(low)
        base = lane // NCOLS + rows(da) + (source - HALO - 1) - start
        place_rows(into, base, size, NCOLS, highs, lows)

    def deposit(source, start, size):
        prepare(coef, source, start, size)
        multiply(acc, start, size, NCOLS, v[pl.ds(source, GROUP)].reshape(KEYS, FIELDS))

    def deposit_sides(sources, *spans):
        many = EDGE_GROUP * NCOLS

        def rows(ref):
            joined = jnp.concatenate([ref[r:r + 1, :] for r in sources], axis=1)
            return jnp.broadcast_to(joined.astype(f32), (16, many)).astype(bf16)
        high, low = split(jnp.concatenate([w[r] for r in sources], axis=1))
        stacked = jnp.concatenate([high, low, rows(da), rows(db)], axis=0)
        row_of, col_of = lane % 128 // 8, lane % 8 + (NCOLS - HALO) * (lane // 128)
        chosen = (lax.broadcasted_iota(i32, (many, KEYS), 0) == row_of * NCOLS + col_of).astype(f32).astype(bf16)
        packed = jnp.dot(stacked, chosen, preferred_element_type=f32)
        step_a, step_b = packed[32:33].astype(i32), packed[48:49].astype(i32)
        target = lax.broadcasted_iota(i32, (16, KEYS), 0)
        target = jnp.where(target < HALO, target - HALO, target + (NCOLS - HALO))
        column = target - (col_of + step_b - 1)
        at = [column == b for b in range(4)]
        kept = []
        for part in (0, 16):
            for a in range(4):
                g = jnp.zeros((16, KEYS), f32)
                for b in range(4):
                    g = jnp.where(at[b], packed[part + 4 * a + b:part + 4 * a + b + 1], g)
                kept.append(g.astype(bf16))
        values = jnp.concatenate(
            [v[r:r + HALO, columns].reshape(KEYS // 4, FIELDS)
             for columns in (left, right) for r in (sources[0], sources[HALO])], axis=0)
        source = jnp.where(row_of < HALO, row_of + sources[0], row_of + (sources[HALO] - HALO))
        for start, size in spans:
            place_rows(coef, source + step_a - (HALO + 1) - start, size, 16, kept[:4], kept[4:])
            multiply(side, start, size, 16, values)

    def sides(start, size, k):
        return [
            to(west, side.at[start:start + size, 0:HALO], side_in.at[1, start:start + size], lon, k),
            to(east, side.at[start:start + size, HALO:2 * HALO], side_in.at[0, start:start + size], lon, k + 1),
        ]

    deposit_sides([HALO + k for k in range(16)], (0, 24))
    deposit_sides([HALO + 16 + k for k in range(16)], (9, 23))
    sideward = sides(8, 16, 0)
    for copy in sideward:
        copy.start()

    @pl.loop(0, 4)
    def _(k):
        deposit(HALO + 8 + 4 * k, 1 + 4 * k, 19)

        @pl.when(jnp.logical_and(k == 2, at_last))
        def _():
            for here, onward in zip(hop_north, on_north):
                here.wait_recv()
                onward.start()

        @pl.when(jnp.logical_and(k == 2, at_first))
        def _():
            for here, onward in zip(hop_south, on_south):
                here.wait_recv()
                onward.start()

    @pl.when(has_south)
    def _():
        for copy in northward[:5]:
            copy.wait_recv()

    @pl.when(has_north)
    def _():
        for copy in southward[:5]:
            copy.wait_recv()

    for m in range(HALO // 2):
        for p, source in ((0, 0), (1, FAR)):
            pair = pack_in[p, m]
            w[source + 2 * m] = pair[:, 0:NCOLS]
            w[source + 2 * m + 1] = pair[:, NCOLS:2 * NCOLS]
    deposit_sides([k for k in range(8)] + [FAR + k for k in range(8)], (0, 8), (24, 8))
    ends = sides(0, 8, 2) + sides(24, 8, 4)
    for copy in ends:
        copy.start()
    sideward += ends
    prepare(last_coef, 0, 0, 4)
    handed = [
        pltpu.make_async_copy(last_coef, coef_out, hand_sem.at[0]),
        pltpu.make_async_copy(v.at[0:4, left], far_out.at[:, left], hand_sem.at[1]),
        pltpu.make_async_copy(v.at[0:4, right], far_out.at[:, right], hand_sem.at[2]),
    ]
    for copy in handed:
        copy.start()
    cleared = pltpu.make_async_copy(v.at[0:4, mid], far_out.at[:, mid], hand_sem.at[3])

    @pl.when(at_first)
    def _():
        cleared.start()

    @pl.loop(0, 2)
    def _(k):
        deposit(HALO + 4 + 20 * k, 16 * k, 16)

    @pl.loop(0, 2)
    def _(k):
        deposit(HALO + 28 * k, 20 * k, 12)

    written = []

    def write(rows, columns):
        copy = pltpu.make_async_copy(acc.at[rows, columns], out_hbm.at[rows, columns], out_sem.at[len(written)])
        copy.start()
        written.append(copy)

    @pl.when(has_north)
    def _():
        southward[5].wait_recv()
        deposit(FAR, 24, 8)

    @pl.when(has_south)
    def _():
        northward[5].wait_recv()
        deposit(4, 0, 8)

    write(slice(0, 28), mid)

    @pl.when(jnp.logical_and(has_north, jnp.logical_not(below)))
    def _():
        south_far.wait_recv()

    @pl.when(below)
    def _():
        for copy in on_south:
            copy.wait_recv()

    @pl.when(has_north)
    def _():
        deposit(FAR + 4, 28, 4)

    write(slice(28, 32), mid)
    for copy in sideward:
        copy.wait_recv()
    acc[:, left] += side_in[0]
    acc[:, right] += side_in[1]
    for columns in (left, right):
        write(slice(0, 32), columns)

    @pl.when(jnp.logical_and(has_south, jnp.logical_not(above)))
    def _():
        north_far.wait_recv()

    @pl.when(above)
    def _():
        for copy in on_north:
            copy.wait_recv()

    @pl.when(has_north)
    def _():
        for copy in northward:
            copy.wait_send()

    @pl.when(has_south)
    def _():
        for copy in southward:
            copy.wait_send()

    @pl.when(jnp.logical_and(has_north, jnp.logical_not(below)))
    def _():
        north_far.wait_send()

    @pl.when(jnp.logical_and(has_south, jnp.logical_not(above)))
    def _():
        south_far.wait_send()

    @pl.when(below)
    def _():
        for copy in hop_north:
            copy.wait_send()

    @pl.when(above)
    def _():
        for copy in hop_south:
            copy.wait_send()

    @pl.when(at_last)
    def _():
        for copy in on_north:
            copy.wait_send()

    @pl.when(at_first)
    def _():
        for copy in on_south:
            copy.wait_send()

    for copy in sideward:
        copy.wait_send()
    for copy in written + handed:
        copy.wait()

    @pl.when(at_first)
    def _():
        cleared.wait()


def finish(total, far, coef, out, near, sem):
    first = pltpu.make_async_copy(total.at[0:4], near, sem.at[0])
    first.start()
    rest = [
        pltpu.make_async_copy(total.at[4 * k:4 * k + 4], out.at[4 * k:4 * k + 4], sem.at[k])
        for k in range(1, NROWS // 4)
    ]
    for copy in rest:
        copy.start()
    values = far[...].reshape(KEYS, FIELDS)
    high = values.astype(bf16)
    low = (values - high.astype(f32)).astype(bf16)
    c = jnp.concatenate([coef[...], coef[:, 0:KEYS]], axis=1)
    added = jnp.dot(c, jnp.concatenate([high, high, low], axis=0), preferred_element_type=f32)
    first.wait()
    near[...] += added.reshape(4, NCOLS, FIELDS)
    last = pltpu.make_async_copy(near, out.at[0:4], sem.at[0])
    last.start()
    for copy in rest + [last]:
        copy.wait()


def body(adj_arrival, weights, dep_lat, dep_lon):
    by_point = jnp.transpose(weights, (0, 2, 1))
    hbm = pl.BlockSpec(memory_space=pl.ANY)
    dma = pltpu.SemaphoreType.DMA
    whole = jax.ShapeDtypeStruct((NROWS, NCOLS, FIELDS), f32)
    total, far, coef = pl.pallas_call(
        kernel,
        out_shape=(
            whole,
            jax.ShapeDtypeStruct((GROUP, NCOLS, FIELDS), f32),
            jax.ShapeDtypeStruct((KEYS, 2 * KEYS), bf16),
        ),
        in_specs=[hbm] * 4,
        out_specs=(hbm, hbm, hbm),
        scratch_shapes=[
            pltpu.VMEM((EXT, NCOLS, FIELDS), f32),
            pltpu.VMEM((EXT, 16, NCOLS), f32),
            pltpu.VMEM((2, HALO // 2, 16, 2 * NCOLS), f32),
            pltpu.VMEM((2, HALO // 2, 16, 2 * NCOLS), f32),
            pltpu.VMEM((EXT, NCOLS), i32),
            pltpu.VMEM((EXT, NCOLS), i32),
            pltpu.VMEM((NROWS, NCOLS, FIELDS), f32),
            pltpu.VMEM((NROWS, 2 * HALO, FIELDS), f32),
            pltpu.VMEM((2, NROWS, HALO, FIELDS), f32),
            pltpu.VMEM((GROUP, NCOLS - 2 * HALO, FIELDS), f32),
            pltpu.VMEM((19 * NCOLS, 2 * KEYS), bf16),
            pltpu.VMEM((KEYS, 2 * KEYS), bf16),
            pltpu.VMEM((2 * KEYS, FIELDS), bf16),
            dma((14,)), dma((14,)), dma((8,)), dma((8,)), dma((6,)), dma((6,)), dma((4,)), dma((4,)), dma((4,)),
        ],
        compiler_params=pltpu.CompilerParams(
            collective_id=0, has_side_effects=True, vmem_limit_bytes=24 << 20),
    )(*(pltpu.with_memory_space_constraint(x, pltpu.HBM) for x in (adj_arrival, by_point, dep_lat, dep_lon)))
    vmem = pl.BlockSpec(memory_space=pltpu.VMEM)
    return pl.pallas_call(
        finish,
        out_shape=whole,
        in_specs=[hbm, vmem, vmem],
        out_specs=hbm,
        scratch_shapes=[pltpu.VMEM((4, NCOLS, FIELDS), f32), dma((NROWS // 4,))],
        compiler_params=pltpu.CompilerParams(vmem_limit_bytes=8 << 20),
    )(total, far, coef)


def solution(mesh):
    placed = (P("lat", "lon", None), P("lat", "lon", None), P("lat", "lon"), P("lat", "lon"))
    return jax.shard_map(
        body, mesh=mesh, in_specs=placed, out_specs=P("lat", "lon", None), check_vma=False
    )
```

```python
import jax
import jax.numpy as jnp
from jax import lax
from jax.experimental import pallas as pl
from jax.experimental.pallas import tpu as pltpu
from jax.sharding import PartitionSpec as P

NROWS, NCOLS, FIELDS = 32, 64, 512
HALO = 8
FAR = HALO + NROWS
EXT = FAR + HALO
GROUP = 4
KEYS = GROUP * NCOLS
EDGE_GROUP = 16
HALF = 256
CROSSING = (
    [(0, 1), (1, 0), (1, 1), (2, 0), (2, 1), (3, 0), (3, 1)],
    [(0, 0), (0, 1), (1, 0), (1, 1), (2, 0), (2, 1), (3, 0)],
)
MESH = pl.DeviceIdType.MESH
f32, bf16, i32 = jnp.float32, jnp.bfloat16, jnp.int32


def kernel(v_hbm, w_hbm, da_hbm, db_hbm, out_hbm, far_out, coef_out,
           v, w, packs, pack_in, da, db, acc, side, side_in, relay, coef, last_coef, rhs,
           lat_send, lat_recv, hop_send, hop_recv, lon_send, lon_recv, own_sem, out_sem, hand_sem):
    nlat, nlon = lax.axis_size("lat"), lax.axis_size("lon")
    half_lat = nlat // 2
    la, lo = lax.axis_index("lat"), lax.axis_index("lon")
    has_south, has_north = la > 0, la < nlat - 1
    at_first, at_last = la == 0, la == nlat - 1
    below, above = la == half_lat - 1, la == half_lat
    at_end, at_middle = jnp.logical_or(at_first, at_last), jnp.logical_or(below, above)
    south, north = {"lat": jnp.maximum(la - 1, 0)}, {"lat": jnp.minimum(la + 1, nlat - 1)}
    east, west = {"lon": lax.rem(lo + 1, nlon)}, {"lon": lax.rem(lo + nlon - 1, nlon)}
    first, last = {"lat": jnp.int32(0)}, {"lat": jnp.int32(nlat - 1)}
    lower, upper = {"lat": jnp.int32(half_lat - 1)}, {"lat": jnp.int32(half_lat)}

    barrier = pltpu.get_barrier_semaphore()

    def greet(device):
        pl.semaphore_signal(barrier, inc=1, device_id=device, device_id_type=MESH)

    greet(east)
    greet(west)

    @pl.when(has_north)
    def _():
        greet(north)

    @pl.when(has_south)
    def _():
        greet(south)

    @pl.when(at_end)
    def _():
        greet(lower)
        greet(upper)

    @pl.when(at_middle)
    def _():
        greet(first)
        greet(last)

    own = [
        pltpu.make_async_copy(v_hbm, v.at[HALO:FAR], own_sem.at[0]),
        pltpu.make_async_copy(w_hbm, w.at[HALO:FAR], own_sem.at[1]),
        pltpu.make_async_copy(da_hbm, da.at[HALO:FAR], own_sem.at[2]),
        pltpu.make_async_copy(db_hbm, db.at[HALO:FAR], own_sem.at[3]),
    ]
    for copy in own:
        copy.start()
    pl.semaphore_wait(
        barrier,
        2 + has_north.astype(i32) + has_south.astype(i32) + 2 * at_end.astype(i32) + 2 * at_middle.astype(i32))

    def to(device, src, dst, sems, k):
        return pltpu.make_async_remote_copy(
            src_ref=src, dst_ref=dst, send_sem=sems[0].at[k], recv_sem=sems[1].at[k],
            device_id=device, device_id_type=MESH)

    lat, hop, lon = (lat_send, lat_recv), (hop_send, hop_recv), (lon_send, lon_recv)
    mid = slice(HALO, NCOLS - HALO)
    left, right = slice(0, HALO), slice(NCOLS - HALO, NCOLS)
    northward = [
        to(north, v_hbm.at[24:32, left], v.at[0:8, left], lat, 0),
        to(north, v_hbm.at[24:32, right], v.at[0:8, right], lat, 1),
        to(north, packs.at[0], pack_in.at[0], lat, 2),
        to(north, v_hbm.at[28:32, mid], v.at[4:8, mid], lat, 5),
    ]
    north_far = to(north, v_hbm.at[24:28, mid], far_out.at[:, mid], lat, 6)
    southward = [
        to(south, v_hbm.at[0:7, left], v.at[FAR:FAR + 7, left], lat, 7),
        to(south, v_hbm.at[0:7, right], v.at[FAR:FAR + 7, right], lat, 8),
        to(south, packs.at[1], pack_in.at[1], lat, 9),
        to(south, v_hbm.at[0:4, mid], v.at[FAR:FAR + 4, mid], lat, 12),
    ]
    south_far = to(south, v_hbm.at[4:7, mid], v.at[FAR + 4:FAR + 7, mid], lat, 13)
    hop_north = [
        to(last, v_hbm.at[26:28, mid], relay.at[2:4], hop, 0),
        to(last, v_hbm.at[24:26, mid], relay.at[0:2], hop, 1),
    ]
    on_north = [
        to(upper, relay.at[2:4], far_out.at[2:4, mid], hop, 2),
        to(upper, relay.at[0:2], far_out.at[0:2, mid], hop, 3),
    ]
    hop_south = [
        to(first, v_hbm.at[4:6, mid], relay.at[0:2], hop, 4),
        to(first, v_hbm.at[6:7, mid], relay.at[2:3], hop, 5),
    ]
    on_south = [
        to(lower, relay.at[0:2], v.at[FAR + 4:FAR + 6, mid], hop, 6),
        to(lower, relay.at[2:3], v.at[FAR + 6:FAR + 7, mid], hop, 7),
    ]

    @pl.when(below)
    def _():
        for copy in hop_north:
            copy.start()

    @pl.when(above)
    def _():
        for copy in hop_south:
            copy.start()

    @pl.when(has_north)
    def _():
        for copy in northward[:2]:
            copy.start()

    @pl.when(has_south)
    def _():
        for copy in southward[:2]:
            copy.start()

    for copy in own[1:]:
        copy.wait()
    for p, source in ((0, FAR - HALO), (1, HALO)):
        for tile, (m, h) in enumerate(CROSSING[p]):
            taps = slice(8 * h, 8 * h + 8)
            packs[p, tile] = jnp.concatenate([w[source + 2 * m, taps], w[source + 2 * m + 1, taps]], axis=1)
        near = slice(source, source + HALO)
        packs[p, 7] = jnp.concatenate([da[near], db[near]], axis=1).astype(f32)

    @pl.when(has_north)
    def _():
        for copy in northward[2:]:
            copy.start()

    @pl.when(has_south)
    def _():
        for copy in southward[2:]:
            copy.start()

    @pl.when(jnp.logical_and(has_north, jnp.logical_not(below)))
    def _():
        north_far.start()

    @pl.when(jnp.logical_and(has_south, jnp.logical_not(above)))
    def _():
        south_far.start()

    v[EXT - 1] = jnp.zeros((NCOLS, FIELDS), f32)

    @pl.when(at_first)
    def _():
        v[0:HALO] = jnp.zeros((HALO, NCOLS, FIELDS), f32)
        pack_in[0] = jnp.zeros((8, 8, 2 * NCOLS), f32)

    @pl.when(at_last)
    def _():
        v[FAR:EXT - 1] = jnp.zeros((HALO - 1, NCOLS, FIELDS), f32)
        pack_in[1] = jnp.zeros((8, 8, 2 * NCOLS), f32)

    acc[...] = jnp.zeros_like(acc)
    side[...] = jnp.zeros_like(side)
    own[0].wait()

    lane = lax.broadcasted_iota(i32, (1, KEYS), 1)

    def split(values):
        high = values.astype(bf16)
        return high, (values - high.astype(f32)).astype(bf16)

    def multiply(total, start, size, width, values):
        rhs[0:KEYS], rhs[KEYS:2 * KEYS] = split(values)
        tall = slice(0, size * width)
        for n in range(FIELDS // HALF):
            part = slice(n * HALF, (n + 1) * HALF)
            c = jnp.concatenate([coef[tall, 0:KEYS], coef[tall, KEYS:2 * KEYS], coef[tall, 0:KEYS]], axis=1)
            r = jnp.concatenate([rhs[0:KEYS, part], rhs[0:KEYS, part], rhs[KEYS:2 * KEYS, part]], axis=0)
            out = jnp.dot(c, r, preferred_element_type=f32)
            total[pl.ds(start, size), :, part] += out.reshape(size, width, HALF)

    def place_rows(into, base, size, width, highs, lows):
        for t in range(size):
            pick = [jnp.broadcast_to((base == t - a).astype(f32), (16, KEYS)).astype(bf16) for a in range(4)]
            pick = [jnp.concatenate([p] * (width // 16), axis=0) for p in pick]
            place = slice(t * width, (t + 1) * width)
            into[place, 0:KEYS] = sum(p * g for p, g in zip(pick, highs))
            into[place, KEYS:2 * KEYS] = sum(p * g for p, g in zip(pick, lows))

    def prepare(into, source, start, size):
        def rows(ref):
            return jnp.concatenate([ref[pl.ds(source + k, 1), :] for k in range(GROUP)], axis=1)
        weights = jnp.concatenate([w[source + k] for k in range(GROUP)], axis=1)
        column = lax.broadcasted_iota(i32, (NCOLS, KEYS), 0) - (lane % NCOLS + rows(db) - 1)
        at = [column == b for b in range(4)]
        highs, lows = [], []
        for a in range(4):
            g = jnp.zeros((NCOLS, KEYS), f32)
            for b in range(4):
                g = jnp.where(at[b], weights[4 * a + b:4 * a + b + 1], g)
            h, low = split(g)
            highs.append(h)
            lows.append(low)
        base = lane // NCOLS + rows(da) + (source - HALO - 1) - start
        place_rows(into, base, size, NCOLS, highs, lows)

    def deposit(source, start, size):
        prepare(coef, source, start, size)
        multiply(acc, start, size, NCOLS, v[pl.ds(source, GROUP)].reshape(KEYS, FIELDS))

    def deposit_sides(sources, *spans):
        many = EDGE_GROUP * NCOLS

        def rows(ref):
            joined = jnp.concatenate([ref[r:r + 1, :] for r in sources], axis=1)
            return jnp.broadcast_to(joined.astype(f32), (16, many)).astype(bf16)
        high, low = split(jnp.concatenate([w[r] for r in sources], axis=1))
        stacked = jnp.concatenate([high, low, rows(da), rows(db)], axis=0)
        row_of, col_of = lane % 128 // 8, lane % 8 + (NCOLS - HALO) * (lane // 128)
        chosen = (lax.broadcasted_iota(i32, (many, KEYS), 0) == row_of * NCOLS + col_of).astype(f32).astype(bf16)
        packed = jnp.dot(stacked, chosen, preferred_element_type=f32)
        step_a, step_b = packed[32:33].astype(i32), packed[48:49].astype(i32)
        target = lax.broadcasted_iota(i32, (16, KEYS), 0)
        target = jnp.where(target < HALO, target - HALO, target + (NCOLS - HALO))
        column = target - (col_of + step_b - 1)
        at = [column == b for b in range(4)]
        kept = []
        for part in (0, 16):
            for a in range(4):
                g = jnp.zeros((16, KEYS), f32)
                for b in range(4):
                    g = jnp.where(at[b], packed[part + 4 * a + b:part + 4 * a + b + 1], g)
                kept.append(g.astype(bf16))
        values = jnp.concatenate(
            [v[r:r + HALO, columns].reshape(KEYS // 4, FIELDS)
             for columns in (left, right) for r in (sources[0], sources[HALO])], axis=0)
        source = jnp.where(row_of < HALO, row_of + sources[0], row_of + (sources[HALO] - HALO))
        for start, size in spans:
            place_rows(coef, source + step_a - (HALO + 1) - start, size, 16, kept[:4], kept[4:])
            multiply(side, start, size, 16, values)

    def sides(start, size, k):
        return [
            to(west, side.at[start:start + size, 0:HALO], side_in.at[1, start:start + size], lon, k),
            to(east, side.at[start:start + size, HALO:2 * HALO], side_in.at[0, start:start + size], lon, k + 1),
        ]

    deposit_sides([HALO + k for k in range(16)], (0, 24))
    deposit_sides([HALO + 16 + k for k in range(16)], (9, 23))
    sideward = sides(8, 16, 0)
    for copy in sideward:
        copy.start()

    @pl.loop(0, 4)
    def _(k):
        deposit(HALO + 8 + 4 * k, 1 + 4 * k, 19)

        @pl.when(jnp.logical_and(k == 2, at_last))
        def _():
            for here, onward in zip(hop_north, on_north):
                here.wait_recv()
                onward.start()

        @pl.when(jnp.logical_and(k == 2, at_first))
        def _():
            for here, onward in zip(hop_south, on_south):
                here.wait_recv()
                onward.start()

    @pl.when(has_south)
    def _():
        for copy in northward[:3]:
            copy.wait_recv()

    @pl.when(has_north)
    def _():
        for copy in southward[:3]:
            copy.wait_recv()

    for p, (source, m, h) in enumerate(((0, 0, 0), (FAR, 3, 1))):
        for k in range(2):
            w[source + 2 * m + k, 8 * h:8 * h + 8] = jnp.zeros((8, NCOLS), f32)
        for tile, (m, h) in enumerate(CROSSING[p]):
            for k in range(2):
                w[source + 2 * m + k, 8 * h:8 * h + 8] = pack_in[p, tile][:, k * NCOLS:(k + 1) * NCOLS]
        near = slice(source, source + HALO)
        da[near] = pack_in[p, 7][:, 0:NCOLS].astype(i32)
        db[near] = pack_in[p, 7][:, NCOLS:2 * NCOLS].astype(i32)
    deposit_sides([k for k in range(8)] + [FAR + k for k in range(8)], (0, 8), (24, 8))
    ends = sides(0, 8, 2) + sides(24, 8, 4)
    for copy in ends:
        copy.start()
    sideward += ends
    prepare(last_coef, 0, 0, 4)
    handed = [
        pltpu.make_async_copy(last_coef, coef_out, hand_sem.at[0]),
        pltpu.make_async_copy(v.at[0:4, left], far_out.at[:, left], hand_sem.at[1]),
        pltpu.make_async_copy(v.at[0:4, right], far_out.at[:, right], hand_sem.at[2]),
    ]
    for copy in handed:
        copy.start()
    cleared = pltpu.make_async_copy(v.at[0:4, mid], far_out.at[:, mid], hand_sem.at[3])

    @pl.when(at_first)
    def _():
        cleared.start()

    @pl.loop(0, 2)
    def _(k):
        deposit(HALO + 4 + 20 * k, 16 * k, 16)

    @pl.loop(0, 2)
    def _(k):
        deposit(HALO + 28 * k, 20 * k, 12)

    written = []

    def write(rows, columns):
        copy = pltpu.make_async_copy(acc.at[rows, columns], out_hbm.at[rows, columns], out_sem.at[len(written)])
        copy.start()
        written.append(copy)

    @pl.when(has_north)
    def _():
        southward[3].wait_recv()
        deposit(FAR, 24, 8)

    @pl.when(has_south)
    def _():
        northward[3].wait_recv()
        deposit(4, 0, 8)

    write(slice(0, 28), mid)

    @pl.when(jnp.logical_and(has_north, jnp.logical_not(below)))
    def _():
        south_far.wait_recv()

    @pl.when(below)
    def _():
        for copy in on_south:
            copy.wait_recv()

    @pl.when(has_north)
    def _():
        deposit(FAR + 4, 28, 4)

    write(slice(28, 32), mid)
    for copy in sideward:
        copy.wait_recv()
    acc[:, left] += side_in[0]
    acc[:, right] += side_in[1]
    for columns in (left, right):
        write(slice(0, 32), columns)

    @pl.when(jnp.logical_and(has_south, jnp.logical_not(above)))
    def _():
        north_far.wait_recv()

    @pl.when(above)
    def _():
        for copy in on_north:
            copy.wait_recv()

    @pl.when(has_north)
    def _():
        for copy in northward:
            copy.wait_send()

    @pl.when(has_south)
    def _():
        for copy in southward:
            copy.wait_send()

    @pl.when(jnp.logical_and(has_north, jnp.logical_not(below)))
    def _():
        north_far.wait_send()

    @pl.when(jnp.logical_and(has_south, jnp.logical_not(above)))
    def _():
        south_far.wait_send()

    @pl.when(below)
    def _():
        for copy in hop_north:
            copy.wait_send()

    @pl.when(above)
    def _():
        for copy in hop_south:
            copy.wait_send()

    @pl.when(at_last)
    def _():
        for copy in on_north:
            copy.wait_send()

    @pl.when(at_first)
    def _():
        for copy in on_south:
            copy.wait_send()

    for copy in sideward:
        copy.wait_send()
    for copy in written + handed:
        copy.wait()

    @pl.when(at_first)
    def _():
        cleared.wait()


def finish(total, far, coef, out, near, sem):
    first = pltpu.make_async_copy(total.at[0:4], near, sem.at[0])
    first.start()
    rest = [
        pltpu.make_async_copy(total.at[4 * k:4 * k + 4], out.at[4 * k:4 * k + 4], sem.at[k])
        for k in range(1, NROWS // 4)
    ]
    for copy in rest:
        copy.start()
    values = far[...].reshape(KEYS, FIELDS)
    high = values.astype(bf16)
    low = (values - high.astype(f32)).astype(bf16)
    c = jnp.concatenate([coef[...], coef[:, 0:KEYS]], axis=1)
    added = jnp.dot(c, jnp.concatenate([high, high, low], axis=0), preferred_element_type=f32)
    first.wait()
    near[...] += added.reshape(4, NCOLS, FIELDS)
    last = pltpu.make_async_copy(near, out.at[0:4], sem.at[0])
    last.start()
    for copy in rest + [last]:
        copy.wait()


def body(adj_arrival, weights, dep_lat, dep_lon):
    by_point = jnp.transpose(weights, (0, 2, 1))
    hbm = pl.BlockSpec(memory_space=pl.ANY)
    dma = pltpu.SemaphoreType.DMA
    whole = jax.ShapeDtypeStruct((NROWS, NCOLS, FIELDS), f32)
    total, far, coef = pl.pallas_call(
        kernel,
        out_shape=(
            whole,
            jax.ShapeDtypeStruct((GROUP, NCOLS, FIELDS), f32),
            jax.ShapeDtypeStruct((KEYS, 2 * KEYS), bf16),
        ),
        in_specs=[hbm] * 4,
        out_specs=(hbm, hbm, hbm),
        scratch_shapes=[
            pltpu.VMEM((EXT, NCOLS, FIELDS), f32),
            pltpu.VMEM((EXT, 16, NCOLS), f32),
            pltpu.VMEM((2, 8, 8, 2 * NCOLS), f32),
            pltpu.VMEM((2, 8, 8, 2 * NCOLS), f32),
            pltpu.VMEM((EXT, NCOLS), i32),
            pltpu.VMEM((EXT, NCOLS), i32),
            pltpu.VMEM((NROWS, NCOLS, FIELDS), f32),
            pltpu.VMEM((NROWS, 2 * HALO, FIELDS), f32),
            pltpu.VMEM((2, NROWS, HALO, FIELDS), f32),
            pltpu.VMEM((GROUP, NCOLS - 2 * HALO, FIELDS), f32),
            pltpu.VMEM((19 * NCOLS, 2 * KEYS), bf16),
            pltpu.VMEM((KEYS, 2 * KEYS), bf16),
            pltpu.VMEM((2 * KEYS, FIELDS), bf16),
            dma((14,)), dma((14,)), dma((8,)), dma((8,)), dma((6,)), dma((6,)), dma((4,)), dma((4,)), dma((4,)),
        ],
        compiler_params=pltpu.CompilerParams(
            collective_id=0, has_side_effects=True, vmem_limit_bytes=24 << 20),
    )(*(pltpu.with_memory_space_constraint(x, pltpu.HBM) for x in (adj_arrival, by_point, dep_lat, dep_lon)))
    vmem = pl.BlockSpec(memory_space=pltpu.VMEM)
    return pl.pallas_call(
        finish,
        out_shape=whole,
        in_specs=[hbm, vmem, vmem],
        out_specs=hbm,
        scratch_shapes=[pltpu.VMEM((4, NCOLS, FIELDS), f32), dma((NROWS // 4,))],
        compiler_params=pltpu.CompilerParams(vmem_limit_bytes=8 << 20),
    )(total, far, coef)


def solution(mesh):
    placed = (P("lat", "lon", None), P("lat", "lon", None), P("lat", "lon"), P("lat", "lon"))
    return jax.shard_map(
        body, mesh=mesh, in_specs=placed, out_specs=P("lat", "lon", None), check_vma=False
    )
```

```python
import jax
import jax.numpy as jnp
from jax import lax
from jax.experimental import pallas as pl
from jax.experimental.pallas import tpu as pltpu
from jax.sharding import PartitionSpec as P

NROWS, NCOLS, FIELDS = 32, 64, 512
HALO = 8
FAR = HALO + NROWS
EXT = FAR + HALO
GROUP = 4
KEYS = GROUP * NCOLS
EDGE_GROUP = 16
HALF = 256
CROSSING = (
    [(0, 1), (1, 0), (1, 1), (2, 0), (2, 1), (3, 0), (3, 1)],
    [(0, 0), (0, 1), (1, 0), (1, 1), (2, 0), (2, 1), (3, 0)],
)
MESH = pl.DeviceIdType.MESH
f32, bf16, i32 = jnp.float32, jnp.bfloat16, jnp.int32


def kernel(v_hbm, w_hbm, da_hbm, db_hbm, out_hbm, far_out, coef_out,
           v, w, packs, pack_in, da, db, acc, side, side_in, relay, coef, last_coef, rhs,
           lat_send, lat_recv, hop_send, hop_recv, lon_send, lon_recv, own_sem, out_sem, hand_sem):
    nlat, nlon = lax.axis_size("lat"), lax.axis_size("lon")
    half_lat = nlat // 2
    la, lo = lax.axis_index("lat"), lax.axis_index("lon")
    has_south, has_north = la > 0, la < nlat - 1
    at_first, at_last = la == 0, la == nlat - 1
    below, above = la == half_lat - 1, la == half_lat
    at_end, at_middle = jnp.logical_or(at_first, at_last), jnp.logical_or(below, above)
    south, north = {"lat": jnp.maximum(la - 1, 0)}, {"lat": jnp.minimum(la + 1, nlat - 1)}
    east, west = {"lon": lax.rem(lo + 1, nlon)}, {"lon": lax.rem(lo + nlon - 1, nlon)}
    first, last = {"lat": jnp.int32(0)}, {"lat": jnp.int32(nlat - 1)}
    lower, upper = {"lat": jnp.int32(half_lat - 1)}, {"lat": jnp.int32(half_lat)}

    barrier = pltpu.get_barrier_semaphore()

    def greet(device):
        pl.semaphore_signal(barrier, inc=1, device_id=device, device_id_type=MESH)

    greet(east)
    greet(west)

    @pl.when(has_north)
    def _():
        greet(north)

    @pl.when(has_south)
    def _():
        greet(south)

    for here, sender in ((at_last, lower), (above, last), (at_first, upper), (below, first)):
        @pl.when(here)
        def _(sender=sender):
            greet(sender)

    own = [
        pltpu.make_async_copy(v_hbm, v.at[HALO:FAR], own_sem.at[0]),
        pltpu.make_async_copy(w_hbm, w.at[HALO:FAR], own_sem.at[1]),
        pltpu.make_async_copy(da_hbm, da.at[HALO:FAR], own_sem.at[2]),
        pltpu.make_async_copy(db_hbm, db.at[HALO:FAR], own_sem.at[3]),
    ]
    for copy in own[1:]:
        copy.start()
    pl.semaphore_wait(
        barrier,
        2 + has_north.astype(i32) + has_south.astype(i32) + at_end.astype(i32) + at_middle.astype(i32))

    def to(device, src, dst, sems, k):
        return pltpu.make_async_remote_copy(
            src_ref=src, dst_ref=dst, send_sem=sems[0].at[k], recv_sem=sems[1].at[k],
            device_id=device, device_id_type=MESH)

    lat, hop, lon = (lat_send, lat_recv), (hop_send, hop_recv), (lon_send, lon_recv)
    mid = slice(HALO, NCOLS - HALO)
    left, right = slice(0, HALO), slice(NCOLS - HALO, NCOLS)
    northward = [
        to(north, v_hbm.at[24:32, left], v.at[0:8, left], lat, 0),
        to(north, v_hbm.at[24:32, right], v.at[0:8, right], lat, 1),
        to(north, packs.at[0], pack_in.at[0], lat, 2),
        to(north, v_hbm.at[28:32, mid], v.at[4:8, mid], lat, 5),
    ]
    north_far = to(north, v_hbm.at[24:28, mid], far_out.at[:, mid], lat, 6)
    southward = [
        to(south, v_hbm.at[0:7, left], v.at[FAR:FAR + 7, left], lat, 7),
        to(south, v_hbm.at[0:7, right], v.at[FAR:FAR + 7, right], lat, 8),
        to(south, packs.at[1], pack_in.at[1], lat, 9),
        to(south, v_hbm.at[0:4, mid], v.at[FAR:FAR + 4, mid], lat, 12),
    ]
    south_far = to(south, v_hbm.at[4:7, mid], v.at[FAR + 4:FAR + 7, mid], lat, 13)
    hop_north = [
        to(last, v_hbm.at[26:28, mid], relay.at[2:4], hop, 0),
        to(last, v_hbm.at[24:26, mid], relay.at[0:2], hop, 1),
    ]
    on_north = [
        to(upper, relay.at[2:4], far_out.at[2:4, mid], hop, 2),
        to(upper, relay.at[0:2], far_out.at[0:2, mid], hop, 3),
    ]
    hop_south = [
        to(first, v_hbm.at[4:6, mid], relay.at[0:2], hop, 4),
        to(first, v_hbm.at[6:7, mid], relay.at[2:3], hop, 5),
    ]
    on_south = [
        to(lower, relay.at[0:2], v.at[FAR + 4:FAR + 6, mid], hop, 6),
        to(lower, relay.at[2:3], v.at[FAR + 6:FAR + 7, mid], hop, 7),
    ]

    @pl.when(below)
    def _():
        for copy in hop_north:
            copy.start()

    @pl.when(above)
    def _():
        for copy in hop_south:
            copy.start()

    @pl.when(has_north)
    def _():
        for copy in northward[:2]:
            copy.start()

    @pl.when(has_south)
    def _():
        for copy in southward[:2]:
            copy.start()

    own[0].start()
    for copy in own[1:]:
        copy.wait()
    for p, source in ((0, FAR - HALO), (1, HALO)):
        for tile, (m, h) in enumerate(CROSSING[p]):
            taps = slice(8 * h, 8 * h + 8)
            packs[p, tile] = jnp.concatenate([w[source + 2 * m, taps], w[source + 2 * m + 1, taps]], axis=1)
        near = slice(source, source + HALO)
        packs[p, 7] = jnp.concatenate([da[near], db[near]], axis=1).astype(f32)

    @pl.when(has_north)
    def _():
        for copy in northward[2:]:
            copy.start()

    @pl.when(has_south)
    def _():
        for copy in southward[2:]:
            copy.start()

    @pl.when(jnp.logical_and(has_north, jnp.logical_not(below)))
    def _():
        north_far.start()

    @pl.when(jnp.logical_and(has_south, jnp.logical_not(above)))
    def _():
        south_far.start()

    v[EXT - 1] = jnp.zeros((NCOLS, FIELDS), f32)

    @pl.when(at_first)
    def _():
        v[0:HALO] = jnp.zeros((HALO, NCOLS, FIELDS), f32)
        pack_in[0] = jnp.zeros((8, 8, 2 * NCOLS), f32)

    @pl.when(at_last)
    def _():
        v[FAR:EXT - 1] = jnp.zeros((HALO - 1, NCOLS, FIELDS), f32)
        pack_in[1] = jnp.zeros((8, 8, 2 * NCOLS), f32)

    acc[...] = jnp.zeros_like(acc)
    side[...] = jnp.zeros_like(side)
    own[0].wait()

    lane = lax.broadcasted_iota(i32, (1, KEYS), 1)

    def split(values):
        high = values.astype(bf16)
        return high, (values - high.astype(f32)).astype(bf16)

    def multiply(total, start, size, width, values):
        rhs[0:KEYS], rhs[KEYS:2 * KEYS] = split(values)
        tall = slice(0, size * width)
        for n in range(FIELDS // HALF):
            part = slice(n * HALF, (n + 1) * HALF)
            c = jnp.concatenate([coef[tall, 0:KEYS], coef[tall, KEYS:2 * KEYS], coef[tall, 0:KEYS]], axis=1)
            r = jnp.concatenate([rhs[0:KEYS, part], rhs[0:KEYS, part], rhs[KEYS:2 * KEYS, part]], axis=0)
            out = jnp.dot(c, r, preferred_element_type=f32)
            total[pl.ds(start, size), :, part] += out.reshape(size, width, HALF)

    def place_rows(into, base, size, width, highs, lows):
        for t in range(size):
            pick = [jnp.broadcast_to((base == t - a).astype(f32), (16, KEYS)).astype(bf16) for a in range(4)]
            pick = [jnp.concatenate([p] * (width // 16), axis=0) for p in pick]
            place = slice(t * width, (t + 1) * width)
            into[place, 0:KEYS] = sum(p * g for p, g in zip(pick, highs))
            into[place, KEYS:2 * KEYS] = sum(p * g for p, g in zip(pick, lows))

    def prepare(into, source, start, size):
        def rows(ref):
            return jnp.concatenate([ref[pl.ds(source + k, 1), :] for k in range(GROUP)], axis=1)
        weights = jnp.concatenate([w[source + k] for k in range(GROUP)], axis=1)
        column = lax.broadcasted_iota(i32, (NCOLS, KEYS), 0) - (lane % NCOLS + rows(db) - 1)
        at = [column == b for b in range(4)]
        highs, lows = [], []
        for a in range(4):
            g = jnp.zeros((NCOLS, KEYS), f32)
            for b in range(4):
                g = jnp.where(at[b], weights[4 * a + b:4 * a + b + 1], g)
            h, low = split(g)
            highs.append(h)
            lows.append(low)
        base = lane // NCOLS + rows(da) + (source - HALO - 1) - start
        place_rows(into, base, size, NCOLS, highs, lows)

    def deposit(source, start, size):
        prepare(coef, source, start, size)
        multiply(acc, start, size, NCOLS, v[pl.ds(source, GROUP)].reshape(KEYS, FIELDS))

    def deposit_sides(sources, *spans):
        many = EDGE_GROUP * NCOLS

        def rows(ref):
            joined = jnp.concatenate([ref[r:r + 1, :] for r in sources], axis=1)
            return jnp.broadcast_to(joined.astype(f32), (16, many)).astype(bf16)
        high, low = split(jnp.concatenate([w[r] for r in sources], axis=1))
        stacked = jnp.concatenate([high, low, rows(da), rows(db)], axis=0)
        row_of, col_of = lane % 128 // 8, lane % 8 + (NCOLS - HALO) * (lane // 128)
        chosen = (lax.broadcasted_iota(i32, (many, KEYS), 0) == row_of * NCOLS + col_of).astype(f32).astype(bf16)
        packed = jnp.dot(stacked, chosen, preferred_element_type=f32)
        step_a, step_b = packed[32:33].astype(i32), packed[48:49].astype(i32)
        target = lax.broadcasted_iota(i32, (16, KEYS), 0)
        target = jnp.where(target < HALO, target - HALO, target + (NCOLS - HALO))
        column = target - (col_of + step_b - 1)
        at = [column == b for b in range(4)]
        kept = []
        for part in (0, 16):
            for a in range(4):
                g = jnp.zeros((16, KEYS), f32)
                for b in range(4):
                    g = jnp.where(at[b], packed[part + 4 * a + b:part + 4 * a + b + 1], g)
                kept.append(g.astype(bf16))
        values = jnp.concatenate(
            [v[r:r + HALO, columns].reshape(KEYS // 4, FIELDS)
             for columns in (left, right) for r in (sources[0], sources[HALO])], axis=0)
        source = jnp.where(row_of < HALO, row_of + sources[0], row_of + (sources[HALO] - HALO))
        for start, size in spans:
            place_rows(coef, source + step_a - (HALO + 1) - start, size, 16, kept[:4], kept[4:])
            multiply(side, start, size, 16, values)

    def sides(start, size, k):
        return [
            to(west, side.at[start:start + size, 0:HALO], side_in.at[1, start:start + size], lon, k),
            to(east, side.at[start:start + size, HALO:2 * HALO], side_in.at[0, start:start + size], lon, k + 1),
        ]

    deposit_sides([HALO + k for k in range(16)], (0, 24))
    deposit_sides([HALO + 16 + k for k in range(16)], (9, 23))
    sideward = sides(8, 16, 0)
    for copy in sideward:
        copy.start()

    @pl.loop(0, 4)
    def _(k):
        deposit(HALO + 8 + 4 * k, 1 + 4 * k, 19)

        @pl.when(jnp.logical_and(k == 2, at_last))
        def _():
            for here, onward in zip(hop_north, on_north):
                here.wait_recv()
                onward.start()

        @pl.when(jnp.logical_and(k == 2, at_first))
        def _():
            for here, onward in zip(hop_south, on_south):
                here.wait_recv()
                onward.start()

    @pl.when(has_south)
    def _():
        for copy in northward[:3]:
            copy.wait_recv()

    @pl.when(has_north)
    def _():
        for copy in southward[:3]:
            copy.wait_recv()

    for p, (source, m, h) in enumerate(((0, 0, 0), (FAR, 3, 1))):
        for k in range(2):
            w[source + 2 * m + k, 8 * h:8 * h + 8] = jnp.zeros((8, NCOLS), f32)
        for tile, (m, h) in enumerate(CROSSING[p]):
            for k in range(2):
                w[source + 2 * m + k, 8 * h:8 * h + 8] = pack_in[p, tile][:, k * NCOLS:(k + 1) * NCOLS]
        near = slice(source, source + HALO)
        da[near] = pack_in[p, 7][:, 0:NCOLS].astype(i32)
        db[near] = pack_in[p, 7][:, NCOLS:2 * NCOLS].astype(i32)
    deposit_sides([k for k in range(8)] + [FAR + k for k in range(8)], (0, 8), (24, 8))
    ends = sides(0, 8, 2) + sides(24, 8, 4)
    for copy in ends:
        copy.start()
    sideward += ends
    prepare(last_coef, 0, 0, 4)
    handed = [
        pltpu.make_async_copy(last_coef, coef_out, hand_sem.at[0]),
        pltpu.make_async_copy(v.at[0:4, left], far_out.at[:, left], hand_sem.at[1]),
        pltpu.make_async_copy(v.at[0:4, right], far_out.at[:, right], hand_sem.at[2]),
    ]
    for copy in handed:
        copy.start()
    cleared = pltpu.make_async_copy(v.at[0:4, mid], far_out.at[:, mid], hand_sem.at[3])

    @pl.when(at_first)
    def _():
        cleared.start()

    @pl.loop(0, 2)
    def _(k):
        deposit(HALO + 4 + 20 * k, 16 * k, 16)

    @pl.loop(0, 2)
    def _(k):
        deposit(HALO + 28 * k, 20 * k, 12)

    written = []

    def write(rows, columns):
        copy = pltpu.make_async_copy(acc.at[rows, columns], out_hbm.at[rows, columns], out_sem.at[len(written)])
        copy.start()
        written.append(copy)

    @pl.when(has_north)
    def _():
        southward[3].wait_recv()
        deposit(FAR, 24, 8)

    @pl.when(has_south)
    def _():
        northward[3].wait_recv()
        deposit(4, 0, 8)

    write(slice(0, 28), mid)

    @pl.when(jnp.logical_and(has_north, jnp.logical_not(below)))
    def _():
        south_far.wait_recv()

    @pl.when(below)
    def _():
        for copy in on_south:
            copy.wait_recv()

    @pl.when(has_north)
    def _():
        deposit(FAR + 4, 28, 4)

    write(slice(28, 32), mid)
    for copy in sideward:
        copy.wait_recv()
    acc[:, left] += side_in[0]
    acc[:, right] += side_in[1]
    for columns in (left, right):
        write(slice(0, 32), columns)

    @pl.when(jnp.logical_and(has_south, jnp.logical_not(above)))
    def _():
        north_far.wait_recv()

    @pl.when(above)
    def _():
        for copy in on_north:
            copy.wait_recv()

    @pl.when(has_north)
    def _():
        for copy in northward:
            copy.wait_send()

    @pl.when(has_south)
    def _():
        for copy in southward:
            copy.wait_send()

    @pl.when(jnp.logical_and(has_north, jnp.logical_not(below)))
    def _():
        north_far.wait_send()

    @pl.when(jnp.logical_and(has_south, jnp.logical_not(above)))
    def _():
        south_far.wait_send()

    @pl.when(below)
    def _():
        for copy in hop_north:
            copy.wait_send()

    @pl.when(above)
    def _():
        for copy in hop_south:
            copy.wait_send()

    @pl.when(at_last)
    def _():
        for copy in on_north:
            copy.wait_send()

    @pl.when(at_first)
    def _():
        for copy in on_south:
            copy.wait_send()

    for copy in sideward:
        copy.wait_send()
    for copy in written + handed:
        copy.wait()

    @pl.when(at_first)
    def _():
        cleared.wait()


def finish(total, far, coef, out, near, sem):
    first = pltpu.make_async_copy(total.at[0:4], near, sem.at[0])
    first.start()
    rest = [
        pltpu.make_async_copy(total.at[4 * k:4 * k + 4], out.at[4 * k:4 * k + 4], sem.at[k])
        for k in range(1, NROWS // 4)
    ]
    for copy in rest:
        copy.start()
    values = far[...].reshape(KEYS, FIELDS)
    high = values.astype(bf16)
    low = (values - high.astype(f32)).astype(bf16)
    c = jnp.concatenate([coef[...], coef[:, 0:KEYS]], axis=1)
    added = jnp.dot(c, jnp.concatenate([high, high, low], axis=0), preferred_element_type=f32)
    first.wait()
    near[...] += added.reshape(4, NCOLS, FIELDS)
    last = pltpu.make_async_copy(near, out.at[0:4], sem.at[0])
    last.start()
    for copy in rest + [last]:
        copy.wait()


def body(adj_arrival, weights, dep_lat, dep_lon):
    by_point = jnp.transpose(weights, (0, 2, 1))
    hbm = pl.BlockSpec(memory_space=pl.ANY)
    dma = pltpu.SemaphoreType.DMA
    whole = jax.ShapeDtypeStruct((NROWS, NCOLS, FIELDS), f32)
    total, far, coef = pl.pallas_call(
        kernel,
        out_shape=(
            whole,
            jax.ShapeDtypeStruct((GROUP, NCOLS, FIELDS), f32),
            jax.ShapeDtypeStruct((KEYS, 2 * KEYS), bf16),
        ),
        in_specs=[hbm] * 4,
        out_specs=(hbm, hbm, hbm),
        scratch_shapes=[
            pltpu.VMEM((EXT, NCOLS, FIELDS), f32),
            pltpu.VMEM((EXT, 16, NCOLS), f32),
            pltpu.VMEM((2, 8, 8, 2 * NCOLS), f32),
            pltpu.VMEM((2, 8, 8, 2 * NCOLS), f32),
            pltpu.VMEM((EXT, NCOLS), i32),
            pltpu.VMEM((EXT, NCOLS), i32),
            pltpu.VMEM((NROWS, NCOLS, FIELDS), f32),
            pltpu.VMEM((NROWS, 2 * HALO, FIELDS), f32),
            pltpu.VMEM((2, NROWS, HALO, FIELDS), f32),
            pltpu.VMEM((GROUP, NCOLS - 2 * HALO, FIELDS), f32),
            pltpu.VMEM((19 * NCOLS, 2 * KEYS), bf16),
            pltpu.VMEM((KEYS, 2 * KEYS), bf16),
            pltpu.VMEM((2 * KEYS, FIELDS), bf16),
            dma((14,)), dma((14,)), dma((8,)), dma((8,)), dma((6,)), dma((6,)), dma((4,)), dma((4,)), dma((4,)),
        ],
        compiler_params=pltpu.CompilerParams(
            collective_id=0, has_side_effects=True, vmem_limit_bytes=24 << 20),
    )(*(pltpu.with_memory_space_constraint(x, pltpu.HBM) for x in (adj_arrival, by_point, dep_lat, dep_lon)))
    vmem = pl.BlockSpec(memory_space=pltpu.VMEM)
    return pl.pallas_call(
        finish,
        out_shape=whole,
        in_specs=[hbm, vmem, vmem],
        out_specs=hbm,
        scratch_shapes=[pltpu.VMEM((4, NCOLS, FIELDS), f32), dma((NROWS // 4,))],
        compiler_params=pltpu.CompilerParams(vmem_limit_bytes=8 << 20),
    )(total, far, coef)


def solution(mesh):
    placed = (P("lat", "lon", None), P("lat", "lon", None), P("lat", "lon"), P("lat", "lon"))
    return jax.shard_map(
        body, mesh=mesh, in_specs=placed, out_specs=P("lat", "lon", None), check_vma=False
    )
```
